32 devices in a mesh: segment: 4 (over y, x), dp: 8 (over z, core).
Axes of the slice: x: 2, y: 2, z: 4, core: 2. Of those that a mesh axis runs over, the one named last changes fastest.
Arguments:
- inputs: bfloat16 [8, 8, 256, 2048], P('segment', 'dp'), may hold values from -6 to 6
- extents: int32 [8, 8, 2], P(None, 'dp'), may hold values from 8 to 16, as said below
- wide_weight: bfloat16 [4, 2048, 512], P('segment'), may hold values from -0.125 to 0.125
- mid_weight: bfloat16 [4, 9, 256, 512], P('segment'), may hold values from -0.09375 to 0.09375
- narrow_gain: bfloat16 [4, 512], P('segment'), may hold values from 0.5 to 1.5
- narrow_bias: bfloat16 [4, 512], P('segment'), may hold values from -3 to 3
- expand_gain: bfloat16 [2048, 2], P('segment'), may hold values from 0.5 to 1.5
- expand_bias: bfloat16 [2048, 2], P('segment'), may hold values from -3 to 3
- head_weight: bfloat16 [2048, 44], P('segment'), may hold values from -0.125 to 0.125
- head_cotangent: bfloat16 [8, 8, 44, 256], P(None, 'dp'), may hold values from -6 to 6
- drop_codes: int32 [8, 8, 2048], P(None, 'dp'), may hold values from 0 to 65535
Outputs:
- logits: float32 [8, 8, 44, 256], P('segment', 'dp')
- input_grad: float32 [8, 8, 256, 2048], P('segment', 'dp')
- wide_grad: float32 [4, 2048, 512], P('segment')
- mid_grad: float32 [4, 9, 256, 512], P('segment')
- narrow_gain_grad: float32 [4, 512], P('segment')
- narrow_bias_grad: float32 [4, 512], P('segment')
- expand_gain_grad: float32 [2048, 2], P('segment')
- expand_bias_grad: float32 [2048, 2], P('segment')
- head_grad: float32 [2048, 44], P('segment')
The draws below stay inside these ranges and needn't reach their ends.
Inputs may be any that keep to these rules, and one draw needn't show every extreme that they name: `extents`: both columns lie in the given range; in every micro-batch some image fills its whole frame.
All inputs are finite; a program needn't handle non-finite values.
Results may differ from the reference program's by a relative error of at most 0.02.
Values may be sent and summed in bfloat16 or wider, within the bound.
No kernel may reach another device: no remote copies, remote signals or barrier semaphores. Data moves between devices by JAX's collectives and lax.ppermute only.
A program may use at most 128 MiB of HBM per device.

```python
import jax
import jax.numpy as jnp
from jax import lax

C = 2048
CB = 512
KSEG = 40
KDEP = 1
KNOR = 3
FRAME = 16
MICRO = 8
KTOT = 44
PIX = 256
IMAGES = 8
N_SEGMENT = 4


def draw_extents(key, part):
    key = jax.random.fold_in(key, 7)
    key_extent, key_choice = jax.random.split(key)
    base_edge = FRAME // 2
    random_bits = jax.random.randint(key_extent, (MICRO, IMAGES, 2), 0, 1 << 20)
    values = base_edge + random_bits % (FRAME - base_edge + 1)
    chosen = jax.random.randint(key_choice, (MICRO, 1), 0, IMAGES)
    picked = jnp.arange(IMAGES, dtype=jnp.int32)[None, :] == chosen
    return jnp.where(picked[:, :, None], FRAME, values).astype(jnp.int32)


def plant(drawn, key, smallest, high):
    dims = drawn.shape
    place = [jax.random.randint(jax.random.fold_in(key, axis), (), 0, dims[axis]) for axis in range(len(dims))]
    drawn = drawn.at[tuple(place)].set(smallest)
    longest = dims.index(max(dims))
    place[longest] = (place[longest] + 1) % dims[longest]
    return drawn.at[tuple(place)].set(high)


def level_of(own_key, shape, cuts, low, high):
    def one(dim, parts):
        steps = jax.random.uniform(jax.random.fold_in(jax.random.fold_in(own_key, 6), dim), (parts,), jnp.float32, low / len(cuts), high / len(cuts))
        return jnp.repeat(jnp.exp(steps), shape[dim] // parts).reshape((-1,) + (1,) * (len(shape) - dim - 1))

    loudness = one(*cuts[0])
    for cut in cuts[1:]:
        loudness = loudness * one(*cut)
    return loudness


def scatter_about(rng, extent, deviation, most, cuts=(), kind=jnp.bfloat16):
    array = deviation * jax.random.normal(rng, extent, jnp.float32)
    if cuts:
        array = array * level_of(rng, extent, cuts, -0.22, 0.18)
    return jnp.clip(array, -most, most).astype(kind)


def setup_inputs(seed: int = 0) -> dict:
    key_of = jax.random.split(jax.random.key(seed), 12)
    return {
        "inputs": scatter_about(key_of[0], (MICRO, IMAGES, PIX, C), 1.0, 6.0, ((0, 4), (1, 8))),
        "extents": draw_extents(jax.random.fold_in(key_of[11], 71), 0),
        "wide_weight": scatter_about(key_of[2], (N_SEGMENT, C, CB), C ** -0.5, 0.125, ((0, 4),)),
        "mid_weight": scatter_about(key_of[3], (N_SEGMENT, 9, CB // 2, CB), (9 * CB) ** -0.5, 0.09375, ((0, 4),)),
        "narrow_gain": jnp.clip(1.0 + 0.1 * jax.random.normal(key_of[4], (N_SEGMENT, CB), jnp.float32), 0.5, 1.5).astype(jnp.bfloat16),
        "narrow_bias": scatter_about(key_of[5], (N_SEGMENT, CB), 0.5, 3.0, ((0, 4),)),
        "expand_gain": jnp.clip(1.0 + 0.1 * jax.random.normal(key_of[6], (C, 2), jnp.float32), 0.5, 1.5).astype(jnp.bfloat16),
        "expand_bias": scatter_about(key_of[7], (C, 2), 0.5, 3.0, ((0, 4),)),
        "head_weight": scatter_about(key_of[8], (C, KTOT), C ** -0.5, 0.125, ((0, 4),)),
        "head_cotangent": scatter_about(key_of[9], (MICRO, IMAGES, KTOT, PIX), 1.0, 6.0, ((1, 8),)),
        "drop_codes": plant(jax.random.randint(key_of[10], (MICRO, IMAGES, C), 0, 65536), jax.random.fold_in(key_of[10], 1), 0, 65535).astype(jnp.int32),
    }


norm_epsilon = 1e-05
drop_floor = 0.01
drop_sharpness = 8.0
code_scale = 65536.0
highest = lax.Precision.HIGHEST

@jax.custom_vjp
def low(v):
    return lax.optimization_barrier(v.astype(jnp.bfloat16)).astype(jnp.float32)

@jax.custom_vjp
def low_back(v):
    return v

def low_keep(v):
    return (low(v), None)

def low_pass(kept, grad):
    return (grad,)

def back_keep(v):
    return (v, None)

def back_low(kept, grad):
    return (low(grad),)
low.defvjp(low_keep, low_pass)
low_back.defvjp(back_keep, back_low)

def pixel_mask(extents):
    position = jnp.arange(FRAME * FRAME, dtype=jnp.int32)
    inside = (position // FRAME < extents[..., 0:1]) & (position % FRAME < extents[..., 1:2])
    return inside.astype(jnp.float32)

def conv_three(source, kernel):
    count_rows = source.shape[0]
    channel_count = source.shape[1]
    framed = source.reshape(count_rows // (FRAME * FRAME), FRAME, FRAME, channel_count)
    padded = jnp.pad(framed, ((0, 0), (1, 1), (1, 1), (0, 0)))
    result = jnp.zeros((count_rows, kernel.shape[-1]), jnp.float32)
    for row_offset in range(3):
        for col_offset in range(3):
            window = padded[:, row_offset:row_offset + FRAME, col_offset:col_offset + FRAME, :].reshape(count_rows, channel_count)
            result = result + jnp.dot(window, kernel[3 * row_offset + col_offset], precision=highest, preferred_element_type=jnp.float32)
    return result

def batch_norm(values, mask_column, pixel_count, norm_gain, norm_bias):
    average = lax.optimization_barrier(jnp.sum(values * mask_column, axis=0)) / pixel_count
    centered = values - average
    variance = lax.optimization_barrier(jnp.sum(centered * centered * mask_column, axis=0)) / pixel_count
    return centered * lax.rsqrt(variance + norm_epsilon) * norm_gain + norm_bias

def bottleneck(entry_rows, mask_column, pixel_count, params, round_entry):
    reduce_weight, head_mid, head_gain, head_bias, expand_weight, tail_mid, tail_gain, tail_bias, out_gain, out_bias = params
    if round_entry:
        entry_rows = low_back(entry_rows)
    residual = low_back(entry_rows)
    first_conv = low_back(jnp.dot(entry_rows, reduce_weight, precision=highest, preferred_element_type=jnp.float32))
    hidden = low(jax.nn.silu(batch_norm(first_conv, mask_column, pixel_count, head_gain, head_bias)) * mask_column)
    half_width = hidden.shape[1] // 2
    upper_part = low_back(hidden[:, half_width:])
    partial_sum = low(conv_three(hidden[:, :half_width], head_mid))
    second_conv = low_back(partial_sum + conv_three(upper_part, tail_mid))
    narrow = low(jax.nn.silu(batch_norm(second_conv, mask_column, pixel_count, tail_gain, tail_bias)) * mask_column)
    third_conv = low_back(lax.dot_general(narrow, expand_weight, (((1,), (1,)), ((), ())), precision=highest, preferred_element_type=jnp.float32))
    summed = batch_norm(third_conv, mask_column, pixel_count, out_gain, out_bias) + residual
    return jax.nn.silu(summed) * mask_column

def trunk_pass(entry_rows, mask_column, pixel_count, wide_all, mid_all, gain_all, bias_all, out_gain_all, out_bias_all):
    first_block = bottleneck(entry_rows, mask_column, pixel_count, (wide_all[0], mid_all[0], gain_all[0], bias_all[0], wide_all[1], mid_all[1], gain_all[1], bias_all[1], out_gain_all[:, 0], out_bias_all[:, 0]), False)
    return bottleneck(low(first_block), mask_column, pixel_count, (wide_all[2], mid_all[2], gain_all[2], bias_all[2], wide_all[3], mid_all[3], gain_all[3], bias_all[3], out_gain_all[:, 1], out_bias_all[:, 1]), True)

def drop_merge(task_grads, thresholds):
    task_total = task_grads[0] + task_grads[1] + task_grads[2]
    magnitude = sum((jnp.sqrt(task_grad * task_grad + drop_floor * drop_floor) for task_grad in task_grads))
    purity = 0.5 * (1.0 + task_total / magnitude)
    keep_share = jax.nn.sigmoid((purity - thresholds) * drop_sharpness)
    merged = jnp.zeros_like(task_total)
    for task_grad in task_grads:
        merged = merged + task_grad * jnp.where(task_grad > 0.0, keep_share, 1.0 - keep_share)
    return merged

def reference(inputs, extents, wide_weight, mid_weight, narrow_gain, narrow_bias, expand_gain, expand_bias, head_weight, head_cotangent, drop_codes):
    params = (wide_weight.astype(jnp.float32), mid_weight.astype(jnp.float32), narrow_gain.astype(jnp.float32), narrow_bias.astype(jnp.float32), expand_gain.astype(jnp.float32), expand_bias.astype(jnp.float32))
    head_all = head_weight.astype(jnp.float32)
    class_index = jnp.arange(KSEG + KDEP + KNOR, dtype=jnp.int32)
    bounds = ((0, KSEG), (KSEG, KSEG + KDEP), (KSEG + KDEP, KSEG + KDEP + KNOR))

    def micro_step(totals, slices):
        batch_input, extent_rows, cotangent, code_block = slices
        mask_rows = pixel_mask(extent_rows)
        mask_column = mask_rows.reshape(-1, 1)
        pixel_count = jnp.sum(mask_rows)
        entry_rows = batch_input.reshape(-1, batch_input.shape[-1]).astype(jnp.float32)

        def forward_pass(entry_arg, wide_arg, mid_arg, gain_arg, bias_arg, out_gain_arg, out_bias_arg):
            return trunk_pass(entry_arg, mask_column, pixel_count, wide_arg, mid_arg, gain_arg, bias_arg, out_gain_arg, out_bias_arg)
        output, pull_trunk = jax.vjp(forward_pass, entry_rows, params[0], params[1], params[2], params[3], params[4], params[5])
        rounded = low(output)

        def project(features, weights):
            return lax.dot_general(weights, features, (((0,), (1,)), ((), ())), precision=highest, preferred_element_type=jnp.float32)
        logits, pull_head = jax.vjp(project, rounded, head_all)
        cotangent_rows = jnp.transpose(cotangent.astype(jnp.float32), (1, 0, 2)).reshape(logits.shape)
        task_grads = [pull_head(cotangent_rows * ((class_index >= range_start) & (class_index < range_stop)).astype(jnp.float32)[:, None])[0] for range_start, range_stop in bounds]
        head_grad = pull_head(cotangent_rows)[1]
        thresholds = (jnp.broadcast_to(code_block[:, None, :], (code_block.shape[0], FRAME * FRAME, code_block.shape[1])).reshape(output.shape).astype(jnp.float32) + 0.5) / code_scale
        merged = drop_merge(task_grads, thresholds)
        trunk_grads = pull_trunk(merged)
        new_totals = jax.tree.map(lambda left_term, right_term: left_term + right_term, totals, tuple(trunk_grads[1:]) + (head_grad,))
        image_logits = jnp.transpose(logits.reshape(logits.shape[0], -1, FRAME * FRAME), (1, 0, 2))
        input_grad = trunk_grads[0].reshape(batch_input.shape)
        return (new_totals, (image_logits, input_grad))
    zero_totals = tuple((jnp.zeros_like(member) for member in params)) + (jnp.zeros_like(head_all),)
    totals, outputs = lax.scan(micro_step, zero_totals, (inputs, extents, head_cotangent, drop_codes))
    return (outputs[0], outputs[1], totals[0], totals[1], totals[2], totals[3], totals[4], totals[5], totals[6])
```

```python
import jax
import jax.numpy as jnp
from jax import lax
from jax.sharding import PartitionSpec as P

KSEG = 40
KDEP = 1
KNOR = 3
FRAME = 16
PIX = FRAME * FRAME
EPS = 1e-05
DROP_FLOOR = 0.01
DROP_SHARPNESS = 8.0
CODE_SCALE = 65536.0
SWAP = 4

f32 = jnp.float32
bf16 = jnp.bfloat16
rows_only = (((0,), (0,)), ((), ()))
last_only = (((1,), (1,)), ((), ()))


def flip(value, bits):
    count = lax.axis_size("dp")
    return lax.ppermute(value, "dp", [(i, i ^ bits) for i in range(count)])


def seg_send(value, pairs):
    return lax.ppermute(value, "segment", pairs)


def group_levels():
    count = lax.axis_size("dp")
    bits = [1 << k for k in range(count.bit_length() - 1)]
    bits = [b for b in bits if b != SWAP]
    levels = [(bits[0], bits[1], bits[0] | bits[1])]
    return levels + [(b,) for b in bits[2:]]


def group_sum(value):
    for level in group_levels():
        got = [flip(value, b) for b in level]
        if len(got) == 3:
            value = (value + got[0]) + (got[1] + got[2])
        else:
            value = value + got[0]
    return value


def group_moments(local_sum, local_square, counts):
    total, square = local_sum, local_square
    for level, parts in zip(group_levels(), counts):
        packed = jnp.stack([total, square])
        got = [packed] + [flip(packed, b) for b in level]
        whole = sum(parts)
        total_next = sum(g[0] for g in got)
        mean = total_next / whole
        square = sum(g[1] for g in got)
        for g, n in zip(got, parts):
            away = g[0] / n - mean
            square = square + away * away * n
        total = total_next
    return mean, lax.rsqrt(square / whole + EPS)


def silu_slope(values):
    part = jax.nn.sigmoid(values)
    return part * (1.0 + values * (1.0 - part))


def patches(source):
    rows, channels = source.shape
    framed = source.reshape(rows // PIX, FRAME, FRAME, channels)
    padded = jnp.pad(framed, ((0, 0), (1, 1), (1, 1), (0, 0)))
    pieces = [
        padded[:, r : r + FRAME, c : c + FRAME, :].reshape(rows, channels)
        for r in range(3)
        for c in range(3)
    ]
    return jnp.concatenate(pieces, axis=-1)


def drop_merge(grads, thresholds):
    total = grads[0] + grads[1] + grads[2]
    magnitude = sum(jnp.sqrt(g * g + DROP_FLOOR * DROP_FLOOR) for g in grads)
    purity = 0.5 * (1.0 + total / magnitude)
    keep = jax.nn.sigmoid((purity - thresholds) * DROP_SHARPNESS)
    merged = jnp.zeros_like(total)
    for g in grads:
        merged = merged + g * jnp.where(g > 0.0, keep, 1.0 - keep)
    return merged


def spread(half, source, segment_index):
    x, y, d = source ^ 1, source ^ 2, source ^ 3
    middle = half.shape[0] // 2
    over_x = seg_send(half, [(source, x)])
    over_y = seg_send(half, [(source, y)])
    upper = seg_send(over_x[:middle], [(x, d)])
    lower = seg_send(over_y[middle:], [(y, d)])
    mine = jnp.where(
        segment_index == source, half, over_x + over_y + jnp.concatenate([upper, lower], axis=0)
    )
    other = flip(mine, 1)
    is_odd = lax.axis_index("dp") % 2 == 1
    return jnp.where(
        is_odd, jnp.concatenate([other, mine], axis=0), jnp.concatenate([mine, other], axis=0)
    )


def my_half(value):
    rows = value.shape[0] // 2
    odd = lax.axis_index("dp") % 2
    return lax.dynamic_slice_in_dim(value, odd * rows, rows, 0)


def gather_back(grad, segment_index):
    rows = grad.shape[0]
    odd = lax.axis_index("dp") % 2
    low = grad.astype(bf16)
    half = rows // 2
    keep = lax.dynamic_slice_in_dim(grad, odd * half, half, 0)
    give = lax.dynamic_slice_in_dim(low, (1 - odd) * half, half, 0)
    summed = keep + flip(give, 1).astype(f32)
    return summed


def on_device(
    inputs,
    extents,
    wide_weight,
    mid_weight,
    narrow_gain,
    narrow_bias,
    expand_gain,
    expand_bias,
    head_weight,
    head_cotangent,
    drop_codes,
):
    seg = lax.axis_index("segment")
    dp = lax.axis_index("dp")
    swapped = (dp // SWAP) % 2
    channels = inputs.shape[-1]
    narrow = wide_weight.shape[-1]
    half_width = narrow // 2
    classes = head_weight.shape[-1]

    def traded(value):
        keep = lax.dynamic_index_in_dim(value, swapped, 0, keepdims=False)
        give = lax.dynamic_index_in_dim(value, 1 - swapped, 0, keepdims=False)
        return jnp.concatenate([keep, flip(give, SWAP)], axis=0)

    own = inputs.shape[0]
    start = seg * own
    entry = traded(inputs).reshape(-1, channels)
    rows = entry.shape[0]
    images = rows // PIX
    box = traded(lax.dynamic_slice_in_dim(extents, start, own, 0))
    cotangent = traded(lax.dynamic_slice_in_dim(head_cotangent, start, own, 0))
    codes = traded(lax.dynamic_slice_in_dim(drop_codes, start, own, 0))

    position = jnp.arange(PIX, dtype=jnp.int32)
    inside = (position // FRAME < box[:, 0:1]) & (position % FRAME < box[:, 1:2])
    mask = inside.astype(f32).reshape(rows, 1)
    local_count = jnp.sum(mask)
    counts = []
    running = local_count
    for level in group_levels():
        parts = [running] + [flip(running, b) for b in level]
        counts.append(parts)
        running = sum(parts)
    pixel_count = running

    packed = jnp.concatenate([expand_gain, expand_bias, head_weight], axis=1).T
    small = lax.all_gather(packed, "segment", axis=1, tiled=True).astype(f32)
    gain_wide, bias_wide = small[0:2], small[2:4]
    head_rows = small[4:].astype(bf16)
    slim = lax.all_gather(jnp.concatenate([narrow_gain, narrow_bias], axis=0), "segment", axis=0)
    gain_narrow = slim[:, 0].astype(f32)
    bias_narrow = slim[:, 1].astype(f32)

    sections = lax.axis_size("segment")
    wide_half = my_half(wide_weight[0])
    mid_half = my_half(mid_weight[0].reshape(-1, narrow))
    order = [("w", 0), ("m", 0), ("m", 1), ("w", 1), ("w", 2), ("m", 2), ("m", 3), ("w", 3)]
    full = {}
    for kind, source in order:
        full[kind, source] = spread(wide_half if kind == "w" else mid_half, source, seg)

    cot_rows = cotangent.transpose(1, 0, 2).reshape(classes, rows)
    bounds = ((0, KSEG), (KSEG, KSEG + KDEP), (KSEG + KDEP, KSEG + KDEP + KNOR))
    thresholds = (
        jnp.broadcast_to(codes[:, None, :], (images, PIX, channels)).reshape(rows, channels).astype(f32)
        + 0.5
    ) / CODE_SCALE
    task_grads = [
        lax.dot_general(cot_rows[a:b], head_rows[a:b], rows_only, preferred_element_type=f32)
        for a, b in bounds
    ]
    merged = drop_merge(task_grads, thresholds)

    def moments(values):
        local_sum = jnp.sum(values * mask, axis=0)
        centered = values - local_sum / local_count
        local_square = jnp.sum(centered * centered * mask, axis=0)
        return group_moments(local_sum, local_square, counts)

    def block_forward(entry, k):
        head, tail = 2 * k, 2 * k + 1
        z1 = jnp.dot(entry, full["w", head], preferred_element_type=f32)
        mean1, inv1 = moments(z1)
        n1 = (z1 - mean1) * inv1
        a1 = n1 * gain_narrow[head] + bias_narrow[head]
        hidden = (jax.nn.silu(a1) * mask).astype(bf16)
        lower, upper = patches(hidden[:, :half_width]), patches(hidden[:, half_width:])
        partial = jnp.dot(lower, full["m", head], preferred_element_type=f32)
        z2 = partial + jnp.dot(upper, full["m", tail], preferred_element_type=f32)
        mean2, inv2 = moments(z2)
        n2 = (z2 - mean2) * inv2
        a2 = n2 * gain_narrow[tail] + bias_narrow[tail]
        hidden2 = (jax.nn.silu(a2) * mask).astype(bf16)
        z3 = lax.dot_general(hidden2, full["w", tail], last_only, preferred_element_type=f32)
        mean3, inv3 = moments(z3)
        n3 = (z3 - mean3) * inv3
        s = n3 * gain_wide[k] + bias_wide[k] + entry.astype(f32)
        out = (jax.nn.silu(s) * mask).astype(bf16)
        return out, (entry, n1, inv1, a1, lower, upper, n2, inv2, a2, hidden2, n3, inv3, s)

    y0, kept0 = block_forward(entry, 0)
    y1, kept1 = block_forward(y0, 1)
    logits = lax.dot_general(head_rows, y1, last_only, preferred_element_type=f32)
    head_grad = lax.dot_general(cot_rows, y1, (((1,), (0,)), ((), ())), preferred_element_type=f32)

    sums = {}
    grads = {}

    def back(d, n, gain, inv, sum_d, sum_dn):
        return (
            mask * inv * (gain * d - (gain * sum_d + n * (gain * sum_dn)) / pixel_count)
        ).astype(bf16)

    def pair_sums(d, n):
        both = group_sum(jnp.stack([jnp.sum(d, axis=0), jnp.sum(d * n, axis=0)]))
        return both

    def conv_back(gradient_patches, kernel):
        flipped = kernel.reshape(9, half_width, narrow)[::-1].transpose(0, 2, 1)
        return jnp.dot(gradient_patches, flipped.reshape(9 * narrow, half_width), preferred_element_type=f32)

    def block_backward(dy, kept, k):
        head, tail = 2 * k, 2 * k + 1
        entry, n1, inv1, a1, lower, upper, n2, inv2, a2, hidden2, n3, inv3, s = kept
        ds = dy * mask * silu_slope(s)
        sums["wide", k] = pair_sums(ds, n3)
        dz3 = back(ds, n3, gain_wide[k], inv3, sums["wide", k][0], sums["wide", k][1])
        dh2 = jnp.dot(dz3, full["w", tail], preferred_element_type=f32)
        grads["w", tail] = lax.dot_general(dz3, hidden2, rows_only, preferred_element_type=f32)
        d2 = dh2 * mask * silu_slope(a2)
        sums["narrow", tail] = pair_sums(d2, n2)
        dz2 = back(d2, n2, gain_narrow[tail], inv2, sums["narrow", tail][0], sums["narrow", tail][1])
        dz2_patches = patches(dz2)
        dh = jnp.concatenate(
            [conv_back(dz2_patches, full["m", head]), conv_back(dz2_patches, full["m", tail])], axis=1
        )
        grads["m", tail] = lax.dot_general(upper, dz2, rows_only, preferred_element_type=f32)
        grads["m", head] = lax.dot_general(lower, dz2, rows_only, preferred_element_type=f32)
        d1 = dh * mask * silu_slope(a1)
        sums["narrow", head] = pair_sums(d1, n1)
        dz1 = back(d1, n1, gain_narrow[head], inv1, sums["narrow", head][0], sums["narrow", head][1])
        grads["w", head] = lax.dot_general(entry, dz1, rows_only, preferred_element_type=f32)
        return lax.dot_general(dz1, full["w", head], last_only, preferred_element_type=f32) + ds

    du1 = block_backward(merged, kept1, 1)
    du0 = block_backward(du1, kept0, 0)

    def reduce_section(kind, source):
        part = gather_back(grads[kind, source], seg)
        x, y, d = source ^ 1, source ^ 2, source ^ 3
        middle = part.shape[0] // 2
        low = part.astype(bf16)
        to_x = seg_send(low[:middle], [(d, x)])
        to_y = seg_send(low[middle:], [(d, y)])
        from_x_lower = seg_send(low[middle:], [(x, source)])
        from_y_upper = seg_send(low[:middle], [(y, source)])
        from_x_upper = seg_send((part[:middle] + to_x.astype(f32)).astype(bf16), [(x, source)])
        from_y_lower = seg_send((part[middle:] + to_y.astype(f32)).astype(bf16), [(y, source)])
        total = part + jnp.concatenate(
            [
                from_y_upper.astype(f32) + from_x_upper.astype(f32),
                from_x_lower.astype(f32) + from_y_lower.astype(f32),
            ],
            axis=0,
        )
        return total

    def all_chips(total):
        count = lax.axis_size("dp")
        bits = [1 << k for k in range(1, count.bit_length() - 1)]
        parts = total
        for b in bits:
            rows_half = parts.shape[0] // 2
            side = (dp // b) % 2
            keep = lax.dynamic_slice_in_dim(parts, side * rows_half, rows_half, 0)
            give = lax.dynamic_slice_in_dim(parts, (1 - side) * rows_half, rows_half, 0).astype(bf16)
            parts = keep + flip(give, b).astype(f32)
        low = parts.astype(bf16)
        for b in bits[::-1] + [1]:
            got = flip(low, b)
            side = (dp // b) % 2 == 1
            low = jnp.where(
                side, jnp.concatenate([got, low], axis=0), jnp.concatenate([low, got], axis=0)
            )
        return low.astype(f32)

    def owned(kind):
        out = None
        for source in range(sections):
            total = reduce_section(kind, source)
            out = total if out is None else jnp.where(seg == source, total, out)
        return all_chips(out)

    wide_grad = owned("w")
    mid_grad = owned("m")

    wide_sums = jnp.stack([sums["wide", 0], sums["wide", 1]])
    narrow_sums = jnp.stack([sums["narrow", i] for i in range(4)])
    flat = jnp.concatenate([wide_sums.reshape(-1, narrow), narrow_sums.reshape(-1, narrow)], axis=0)
    flat = flat + flip(flat, SWAP)
    flat = flat + seg_send(flat, [(i, i ^ 1) for i in range(sections)])
    flat = flat + seg_send(flat, [(i, i ^ 2) for i in range(sections)])
    wide_count = wide_sums.size // narrow
    wide_all = flat[:wide_count].reshape(2, 2, channels)
    narrow_all = lax.dynamic_index_in_dim(flat[wide_count:].reshape(sections, 2, narrow), seg, 0, keepdims=False)
    share = channels // sections
    wide_mine = lax.dynamic_slice_in_dim(wide_all, seg * share, share, 2)

    head_part = lax.psum_scatter(head_grad, "segment", scatter_dimension=1, tiled=True)
    head_out = lax.psum(head_part, "dp").T

    def returned(value):
        keep = value[: images // 2]
        got = flip(value[images // 2 :].astype(bf16), SWAP).astype(f32)
        first = jnp.where(swapped == 0, keep, got)
        second = jnp.where(swapped == 0, got, keep)
        return jnp.stack([first, second])

    logits_out = returned(logits.reshape(classes, images, PIX).transpose(1, 0, 2))
    input_grad = returned(du0.reshape(images, PIX, channels))

    return (
        logits_out,
        input_grad,
        wide_grad[None],
        mid_grad.reshape(1, 9, half_width, narrow),
        narrow_all[1:2],
        narrow_all[0:1],
        wide_mine[:, 1].T,
        wide_mine[:, 0].T,
        head_out,
    )


def solution(mesh):
    return jax.shard_map(
        on_device,
        mesh=mesh,
        in_specs=(
            P("segment", "dp", None, None),
            P(None, "dp", None),
            P("segment", None, None),
            P("segment", None, None, None),
            P("segment", None),
            P("segment", None),
            P("segment", None),
            P("segment", None),
            P("segment", None),
            P(None, "dp", None, None),
            P(None, "dp", None),
        ),
        out_specs=(
            P("segment", "dp", None, None),
            P("segment", "dp", None, None),
            P("segment", None, None),
            P("segment", None, None, None),
            P("segment", None),
            P("segment", None),
            P("segment", None),
            P("segment", None),
            P("segment", None),
        ),
        check_vma=False,
    )
```

```python
import functools

import jax
import jax.numpy as jnp
from jax import lax
from jax.experimental import pallas as pl
from jax.experimental.pallas import tpu as pltpu
from jax.sharding import PartitionSpec as P

KSEG = 40
KDEP = 1
KNOR = 3
FRAME = 16
PIX = FRAME * FRAME
EPS = 1e-05
DROP_FLOOR = 0.01
DROP_SHARPNESS = 8.0
CODE_SCALE = 65536.0
SWAP = 2
STEP = 64
PAD = FRAME
HEADS = 64
LIMIT = 24 << 20

f32 = jnp.float32
bf16 = jnp.bfloat16
rows_only = (((0,), (0,)), ((), ()))
last_only = (((1,), (1,)), ((), ()))


def sigmoid(values):
    return 0.5 * jnp.tanh(0.5 * values) + 0.5


def fold(values):
    return jnp.sum(values.reshape(values.shape[0] // 8, 8, values.shape[1]), axis=0)


def over_rows(rows, body, init):
    def one(index, carry):
        return body(pl.ds(pl.multiple_of(index * STEP, STEP), STEP), carry)

    return lax.fori_loop(0, rows // STEP, one, init)


def column_sum(total):
    return jnp.sum(total, axis=0, keepdims=True)


def local_moments(z_ref, cols, mask_ref, count, st_ref):
    rows, width = z_ref.shape[0], cols.size
    zero = jnp.zeros((8, width), f32)

    def add(r, total):
        return total + fold(z_ref[r, cols] * mask_ref[r, :])

    total = column_sum(over_rows(rows, add, zero))
    mean = total / count

    def add_square(r, square):
        away = z_ref[r, cols] - mean
        return square + fold(away * away * mask_ref[r, :])

    square = column_sum(over_rows(rows, add_square, zero))
    st_ref[0:1, cols] = total
    st_ref[1:2, cols] = square
    if st_ref.shape[0] > 2:
        st_ref[2:3, cols] = jnp.zeros_like(total) + count


def pixels(counts):
    numbers = [c[0:1, 0:1] for c in counts]
    return numbers, (numbers[0] + numbers[1]) + (numbers[2] + numbers[3])


def merged_moments(parts, counts, mi_ref):
    numbers, whole = pixels(counts)
    sums = [p[0:1, :] for p in parts]
    squares = [p[1:2, :] for p in parts]
    mean = ((sums[0] + sums[1]) + (sums[2] + sums[3])) / whole
    square = (squares[0] + squares[1]) + (squares[2] + squares[3])
    for s, n in zip(sums, numbers):
        away = s / n - mean
        square = square + away * away * n
    mi_ref[0:1, :] = mean
    mi_ref[1:2, :] = lax.rsqrt(square / whole + EPS)


def merged_sums(parts, out_ref):
    out_ref[...] = (parts[0][...] + parts[1][...]) + (parts[2][...] + parts[3][...])


class Weights:
    def __init__(self, section, place_ref, sources, buffer, sems):
        self.buffer, self.sems = buffer, sems
        self.piece = buffer.shape[0] // 4
        self.own = own = sources[0]
        first, second, third, other_first, other_second, other_third = sources[1:]
        relative = place_ref[0] ^ section
        core = place_ref[1]
        straight = relative == 1 + core
        near = (relative == 1) | (relative == 2)

        @pl.when(relative == 0)
        def _():
            for i in range(4):
                pltpu.make_async_copy(own.at[pl.ds(i * self.piece, self.piece)], self.part(i), sems.at[i]).start()

        def fetch(mine, other):
            for i in range(4):
                source, side = (mine, core) if i < 2 else (other, 1 - core)
                at = side * 2 + i % 2
                rows = pl.ds(i % 2 * self.piece, self.piece)
                pltpu.make_async_copy(source.at[rows], self.part(at), sems.at[at]).start()

        @pl.when(near & straight)
        def _():
            fetch(first, other_second)

        @pl.when(near & jnp.logical_not(straight))
        def _():
            fetch(second, other_first)

        @pl.when(relative == 3)
        def _():
            fetch(third, other_third)

    def part(self, at):
        start = at * self.piece
        if not isinstance(at, int):
            start = pl.multiple_of(start, 16)
        return self.buffer.at[pl.ds(start, self.piece)]

    def wait(self, at):
        source = self.own.at[pl.ds(0, self.piece)]
        pltpu.make_async_copy(source, self.part(at), self.sems.at[at]).wait()


def blocks(width, count=4):
    size = width // count
    return [pl.ds(i * size, size) for i in range(count)]


def first_kernel(section, place, k0, u, mask, *rest):
    sources, (z, st, w, sems) = rest[:7], rest[7:]
    weights = Weights(section, place, sources, w, sems)
    for i, cols in enumerate(blocks(u.shape[1])):
        weights.wait(i)
        part = jnp.dot(u[:, cols], w[cols, :], preferred_element_type=f32)
        z[...] = part if i == 0 else z[...] + part
    local_moments(z, pl.ds(0, z.shape[1]), mask, k0[0:1, 0:1], st)


def shifted_copies(values, column):
    left = jnp.where(column >= 1, pltpu.roll(values, 1, 0), 0.0)
    right = jnp.where(column < FRAME - 1, pltpu.roll(values, PIX - 1, 0), 0.0)
    return left, values, right


def clear_borders(buffer):
    images, rows, width = buffer.shape
    zero = jnp.zeros((images, PAD, width), bf16)
    buffer[:, 0:PAD, :] = zero
    buffer[:, rows - PAD : rows, :] = zero


def frame_column(width):
    return lax.broadcasted_iota(jnp.int32, (PIX, width), 0) % FRAME


def middle_kernel(section, place, k0, k1, k2, k3, z1, p0, p1, p2, p3, gain, bias, mask, *rest):
    sources, (hs, z2, st, mi, ka, kt, sems_a, sems_t) = rest[:7], rest[7:]
    lower = Weights(section, place, sources, ka, sems_a)
    upper = Weights(section + 1, place, sources, kt, sems_t)
    merged_moments((p0, p1, p2, p3), (k0, k1, k2, k3), mi)
    clear_borders(hs)
    images = hs.shape[0]
    half = z1.shape[1] // 2
    column = frame_column(128)

    def one(image, carry):
        r = pl.ds(pl.multiple_of(image * PIX, PIX), PIX)
        for j in range(z1.shape[1] // 128):
            cols = pl.ds(j * 128, 128)
            n = (z1[r, cols] - mi[0:1, cols]) * mi[1:2, cols]
            a = n * gain[:, cols] + bias[:, cols]
            h = a * sigmoid(a) * mask[r, :]
            side, inner = divmod(j * 128, half)
            for k, copy in enumerate(shifted_copies(h, column)):
                hs[image, PAD : PAD + PIX, pl.ds(side * 3 * half + k * half + inner, 128)] = copy.astype(bf16)
        return carry

    lax.fori_loop(0, images, one, 0)
    for weights in (lower, upper):
        for i in range(4):
            weights.wait(i)
    rows = z1.shape[0]
    for d in range(3):
        taps = hs[:, FRAME * d : FRAME * d + PIX, :].reshape(rows, 6 * half)
        ks = pl.ds(3 * half * d, 3 * half)
        part = jnp.dot(taps[:, : 3 * half], ka[ks, :], preferred_element_type=f32)
        part = part + jnp.dot(taps[:, 3 * half :], kt[ks, :], preferred_element_type=f32)
        z2[...] = part if d == 0 else z2[...] + part
    local_moments(z2, pl.ds(0, z2.shape[1]), mask, k0[0:1, 0:1], st)


def expand_kernel(section, place, k0, k1, k2, k3, z2, p0, p1, p2, p3, gain, bias, mask, *rest):
    sources, (h2, z3, st, mi, w, sems) = rest[:7], rest[7:]
    weights = Weights(section, place, sources, w, sems)
    merged_moments((p0, p1, p2, p3), (k0, k1, k2, k3), mi)

    def one(r, carry):
        n = (z2[r, :] - mi[0:1, :]) * mi[1:2, :]
        a = n * gain[...] + bias[...]
        h2[r, :] = (a * sigmoid(a) * mask[r, :]).astype(bf16)
        return carry

    over_rows(z2.shape[0], one, 0)
    for i, cols in enumerate(blocks(z3.shape[1])):
        weights.wait(i)
        z3[:, cols] = lax.dot_general(h2[...], w[cols, :], last_only, preferred_element_type=f32)
        local_moments(z3, cols, mask, k0[0:1, 0:1], st)


def join_kernel(section, place, k0, k1, k2, k3, z3, p0, p1, p2, p3, gain, bias, u, mask, *rest):
    sources, (y, z, st, mi, w, sems) = rest[:7], rest[7:]
    weights = Weights(section, place, sources, w, sems)
    merged_moments((p0, p1, p2, p3), (k0, k1, k2, k3), mi)
    for i, cols in enumerate(blocks(z3.shape[1])):

        def one(r, carry, cols=cols):
            n = (z3[r, cols] - mi[0:1, cols]) * mi[1:2, cols]
            s = n * gain[:, cols] + bias[:, cols] + u[r, cols].astype(f32)
            y[r, cols] = (s * sigmoid(s) * mask[r, :]).astype(bf16)
            return carry

        over_rows(z3.shape[0], one, 0)
        weights.wait(i)
        part = jnp.dot(y[:, cols], w[cols, :], preferred_element_type=f32)
        z[...] = part if i == 0 else z[...] + part
    local_moments(z, pl.ds(0, z.shape[1]), mask, k0[0:1, 0:1], st)


def slope_of(s):
    part = sigmoid(s)
    return part, part * (1.0 + s * (1.0 - part))


def turn_kernel(k0, k1, k2, k3, z3, p0, p1, p2, p3, gain, bias, u, mask, merged, head, cot, ds, n3, sums, logits, hgrad, mi, y):
    merged_moments((p0, p1, p2, p3), (k0, k1, k2, k3), mi)
    for i, cols in enumerate(blocks(z3.shape[1])):
        width = cols.size

        def one(r, carry, cols=cols):
            n = (z3[r, cols] - mi[0:1, cols]) * mi[1:2, cols]
            s = n * gain[:, cols] + bias[:, cols] + u[r, cols].astype(f32)
            part, slope = slope_of(s)
            y[r, :] = (s * part * mask[r, :]).astype(bf16)
            d = merged[r, cols].astype(f32) * mask[r, :] * slope
            ds[r, cols] = d.astype(bf16)
            n3[r, cols] = n.astype(bf16)
            return carry[0] + fold(d), carry[1] + fold(d * n)

        zero = jnp.zeros((8, width), f32)
        both = over_rows(z3.shape[0], one, (zero, zero))
        sums[0:1, cols] = column_sum(both[0])
        sums[1:2, cols] = column_sum(both[1])
        part = lax.dot_general(head[:, cols], y[...], last_only, preferred_element_type=f32)
        logits[...] = part if i == 0 else logits[...] + part
        for image in range(cot.shape[0]):
            r = pl.ds(image * PIX, PIX)
            part = jnp.dot(cot[image], y[r, :], preferred_element_type=f32)
            hgrad[:, cols] = part if image == 0 else hgrad[:, cols] + part


def shrink_kernel(section, place, number, ds, n3, q0, q1, q2, q3, mi3, gain3, mask, z2, mi2, gain2, bias2, *rest):
    sources, (dz3, d2, sums, tot, w, sems) = rest[:7], rest[7:]
    weights = Weights(section, place, sources, w, sems)
    merged_sums((q0, q1, q2, q3), tot)
    for i, cols in enumerate(blocks(ds.shape[1])):
        g = gain3[:, cols] * mi3[1:2, cols]
        c1 = g * tot[0:1, cols] / number[0:1, 0:1]
        c2 = g * tot[1:2, cols] / number[0:1, 0:1]

        def one(r, carry, cols=cols, g=g, c1=c1, c2=c2):
            d = g * ds[r, cols].astype(f32) - (c1 + n3[r, cols].astype(f32) * c2)
            dz3[r, cols] = (mask[r, :] * d).astype(bf16)
            return carry

        over_rows(ds.shape[0], one, 0)
        weights.wait(i)
        part = jnp.dot(dz3[:, cols], w[cols, :], preferred_element_type=f32)
        d2[...] = part if i == 0 else d2[...] + part
    narrow_back(d2, z2, mi2, gain2, bias2, mask, sums)


def narrow_back(d, z, mi, gain, bias, mask, sums):
    zero = jnp.zeros((8, z.shape[1]), f32)

    def one(r, carry):
        n = (z[r, :] - mi[0:1, :]) * mi[1:2, :]
        slope = slope_of(n * gain[...] + bias[...])[1]
        value = d[r, :] * mask[r, :] * slope
        d[r, :] = value
        return carry[0] + fold(value), carry[1] + fold(value * n)

    both = over_rows(z.shape[0], one, (zero, zero))
    sums[0:1, :] = column_sum(both[0])
    sums[1:2, :] = column_sum(both[1])


def unmix_kernel(section, place, number, d2, q0, q1, q2, q3, z2, mi2, gain2, mask, z1, mi1, gain1, bias1, *rest):
    sources, (dz2, d1, sums, tot, gs, ka, kt, sems_a, sems_t) = rest[:7], rest[7:]
    lower = Weights(section, place, sources, ka, sems_a)
    upper = Weights(section + 1, place, sources, kt, sems_t)
    merged_sums((q0, q1, q2, q3), tot)
    clear_borders(gs)
    images = gs.shape[0]
    rows, width = z2.shape
    half = width // 2
    column = frame_column(128)

    def one(image, carry):
        r = pl.ds(pl.multiple_of(image * PIX, PIX), PIX)
        for j in range(width // 128):
            cols = pl.ds(j * 128, 128)
            g = gain2[:, cols] * mi2[1:2, cols]
            c1 = g * tot[0:1, cols] / number[0:1, 0:1]
            c2 = g * tot[1:2, cols] / number[0:1, 0:1]
            n = (z2[r, cols] - mi2[0:1, cols]) * mi2[1:2, cols]
            d = mask[r, :] * (g * d2[r, cols] - (c1 + n * c2))
            dz2[r, cols] = d.astype(bf16)
            for k, copy in enumerate(shifted_copies(d, column)):
                gs[image, PAD : PAD + PIX, pl.ds(k * width + j * 128, 128)] = copy.astype(bf16)
        return carry

    lax.fori_loop(0, images, one, 0)
    for weights in (lower, upper):
        for i in range(4):
            weights.wait(i)
    for d in range(3):
        for k in range(3):
            moved = gs[:, FRAME * (2 - d) : FRAME * (2 - d) + PIX, pl.ds((2 - k) * width, width)]
            moved = moved.reshape(rows, width)
            tap = pl.ds((3 * d + k) * half, half)
            for side, kernel in enumerate((ka, kt)):
                cols = pl.ds(side * half, half)
                part = lax.dot_general(moved, kernel[tap, :], last_only, preferred_element_type=f32)
                d1[:, cols] = part if d + k == 0 else d1[:, cols] + part
    narrow_back(d1, z1, mi1, gain1, bias1, mask, sums)


def narrow_finish(d1, q, z1, mi1, gain1, mask, number, dz1, tot):
    merged_sums(q, tot)
    g = gain1[...] * mi1[1:2, :]
    c1 = g * tot[0:1, :] / number[0:1, 0:1]
    c2 = g * tot[1:2, :] / number[0:1, 0:1]

    def one(r, carry):
        n = (z1[r, :] - mi1[0:1, :]) * mi1[1:2, :]
        dz1[r, :] = (mask[r, :] * (g * d1[r, :] - (c1 + n * c2))).astype(bf16)
        return carry

    over_rows(z1.shape[0], one, 0)


def widen_kernel(section, place, number, d1, q0, q1, q2, q3, z1, mi1, gain1, mask, ds, z3, mi3, gain3, bias3, u, *rest):
    sources, (dz1, ds0, n3, sums, tot, w, du, sems) = rest[:7], rest[7:]
    weights = Weights(section, place, sources, w, sems)
    narrow_finish(d1, (q0, q1, q2, q3), z1, mi1, gain1, mask, number, dz1, tot)
    for i, cols in enumerate(blocks(ds.shape[1])):
        weights.wait(i)
        du[...] = lax.dot_general(dz1[...], w[cols, :], last_only, preferred_element_type=f32)

        def one(r, carry, cols=cols):
            dy = (du[r, :] + ds[r, cols].astype(f32)).astype(bf16).astype(f32)
            n = (z3[r, cols] - mi3[0:1, cols]) * mi3[1:2, cols]
            s = n * gain3[:, cols] + bias3[:, cols] + u[r, cols].astype(f32)
            d = dy * mask[r, :] * slope_of(s)[1]
            ds0[r, cols] = d.astype(bf16)
            n3[r, cols] = n.astype(bf16)
            return carry[0] + fold(d), carry[1] + fold(d * n)

        zero = jnp.zeros((8, cols.size), f32)
        both = over_rows(ds.shape[0], one, (zero, zero))
        sums[0:1, cols] = column_sum(both[0])
        sums[1:2, cols] = column_sum(both[1])


def last_kernel(section, place, number, d1, q0, q1, q2, q3, z1, mi1, gain1, mask, ds, *rest):
    sources, (dz1, keep, give, tot, w, sems) = rest[:7], rest[7:]
    weights = Weights(section, place, sources, w, sems)
    narrow_finish(d1, (q0, q1, q2, q3), z1, mi1, gain1, mask, number, dz1, tot)
    half = keep.shape[0]
    for i, cols in enumerate(blocks(ds.shape[1])):
        weights.wait(i)
        block = lax.dot_general(dz1[...], w[cols, :], last_only, preferred_element_type=f32)
        keep[:, cols] = block[:half] + ds[:half, cols].astype(f32)
        give[:, cols] = (block[half:] + ds[half:, cols].astype(f32)).astype(bf16)


def drop_kernel(codes, cots, head, merged):
    line = lax.broadcasted_iota(jnp.int32, cots.shape[1:], 0)
    bounds = (0, KSEG, KSEG + KDEP, KSEG + KDEP + KNOR)
    cot = cots[0].astype(f32)
    tasks = [
        jnp.where((line >= a) & (line < b), cot, 0.0).T.astype(bf16)
        for a, b in zip(bounds[:-1], bounds[1:])
    ]
    for cols in blocks(head.shape[1], 8):
        g = [jnp.dot(task, head[:, cols], preferred_element_type=f32) for task in tasks]
        total = g[0] + g[1] + g[2]
        magnitude = sum(jnp.sqrt(v * v + DROP_FLOOR * DROP_FLOOR) for v in g)
        purity = 0.5 + 0.5 * (total / magnitude)
        bar = (codes[0, :, cols] + 0.5) / CODE_SCALE
        keep = sigmoid((purity - bar) * DROP_SHARPNESS)
        lose = 1.0 - keep
        value = sum(v * jnp.where(v > 0.0, keep, lose) for v in g)
        merged[:, cols] = value.astype(bf16)


VM = pl.BlockSpec(memory_space=pltpu.VMEM)
SM = pl.BlockSpec(memory_space=pltpu.SMEM)
ANY = pl.BlockSpec(memory_space=pltpu.HBM)


def run(kernel, operands, specs, outs, scratch, flops):
    return pl.pallas_call(
        kernel,
        out_shape=[jax.ShapeDtypeStruct(shape, kind) for shape, kind in outs],
        in_specs=specs,
        out_specs=[VM] * len(outs),
        scratch_shapes=scratch,
        compiler_params=pltpu.CompilerParams(vmem_limit_bytes=LIMIT),
        cost_estimate=pl.CostEstimate(
            flops=flops,
            bytes_accessed=sum(o.size * o.dtype.itemsize for o in operands[:16]),
            transcendentals=0,
        ),
    )(*operands)


def flip(value, bits):
    count = lax.axis_size("dp")
    return lax.ppermute(value, "dp", [(i, i ^ bits) for i in range(count)])


def cross(value, bits):
    count = lax.axis_size("segment")
    return lax.ppermute(value, "segment", [(i, i ^ bits) for i in range(count)])


def turned(value, even, odd):
    size, count = lax.axis_size("segment"), lax.axis_size("dp")
    pairs = [
        (i * count + j, (i ^ (odd if j % 2 else even)) * count + j) for i in range(size) for j in range(count)
    ]
    return lax.ppermute(value, ("segment", "dp"), pairs)


def after(value, *others):
    return lax.optimization_barrier((value,) + others)[0]


def dp_bits():
    count = lax.axis_size("dp")
    return [1 << k for k in range(count.bit_length() - 1)]


def group_bits():
    bits = [b for b in dp_bits() if b != SWAP]
    return bits[:2], bits[2:]


def four_parts(value):
    first, _ = group_bits()
    near = jnp.stack([value, flip(value, first[0])])
    far = flip(near, first[1])
    return [near[0], near[1], far[0], far[1]]


def pair_up(stats, count):
    for b in group_bits()[1]:
        other, other_count = flip(stats, b), flip(count, b)
        whole = count + other_count
        here, there = count[0, 0], other_count[0, 0]
        away = stats[0] / here - other[0] / there
        square = stats[1] + other[1] + away * away * (here * there / (here + there))
        merged = jnp.stack([stats[0] + other[0], square])
        if stats.shape[0] > 2:
            merged = jnp.concatenate([merged, stats[2:] + other[2:]], axis=0)
        stats, count = merged, whole
    return stats


def pair_sum(value):
    for b in group_bits()[1]:
        value = value + flip(value, b)
    return value


def split_rows(value, index, parts=2):
    size = value.shape[0] // parts
    return lax.dynamic_slice_in_dim(value, index * size, size, 0)


def on_device(
    inputs,
    extents,
    wide_weight,
    mid_weight,
    narrow_gain,
    narrow_bias,
    expand_gain,
    expand_bias,
    head_weight,
    head_cotangent,
    drop_codes,
):
    seg = lax.axis_index("segment")
    dp = lax.axis_index("dp")
    sections = lax.axis_size("segment")
    x_side, y_side, core = seg % 2, seg // 2, dp % 2
    swapped = (dp // SWAP) % 2
    channels = inputs.shape[-1]
    narrow = wide_weight.shape[-1]
    half_width = narrow // 2
    classes = head_weight.shape[-1]
    place = jnp.stack([seg, core]).astype(jnp.int32)

    own_small = jnp.concatenate(
        [head_weight.T, jnp.zeros((HEADS - classes, head_weight.shape[0]), bf16), expand_gain.T, expand_bias.T]
        + [narrow_gain, narrow_bias, jnp.zeros((10, narrow), bf16)],
        axis=0,
    )
    small_x = cross(own_small, 1)
    small_y = cross(jnp.stack([own_small, small_x]), 2)
    small = jnp.stack([own_small, small_x, small_y[0], small_y[1]])
    small = jnp.stack([lax.dynamic_index_in_dim(small, k ^ seg, 0, keepdims=False) for k in range(4)])
    lanes = jnp.moveaxis(small[:, : HEADS + 4], 0, 1).reshape(HEADS + 4, channels)
    head_rows = lanes[:HEADS]
    gain_wide = lanes[HEADS : HEADS + 2].astype(f32)
    bias_wide = lanes[HEADS + 2 : HEADS + 4].astype(f32)
    gain_narrow = small[:, HEADS + 4].astype(f32)
    bias_narrow = small[:, HEADS + 5].astype(f32)

    own_count = inputs.shape[0]
    start = seg * own_count

    def own_part(value):
        return lax.dynamic_slice_in_dim(value, start, own_count, 0).astype(f32).reshape(own_count, -1, PIX)

    boxes = jnp.pad(extents, ((0, 0), (0, 0), (0, PIX - 2)))
    facts = jnp.concatenate([own_part(v) for v in (head_cotangent, drop_codes, boxes)], axis=1)
    facts = jnp.pad(facts, ((0, 0), (0, -facts.shape[1] % 8), (0, 0)))
    keep_facts = lax.dynamic_index_in_dim(facts, swapped, 0, keepdims=False)
    got_facts = flip(lax.dynamic_index_in_dim(facts, 1 - swapped, 0, keepdims=False), SWAP)
    facts = jnp.stack([keep_facts, got_facts])
    code_rows = channels // PIX
    cotangent = facts[:, :classes].astype(bf16)
    codes = facts[:, classes : classes + code_rows].reshape(2, 1, channels)
    box = facts[:, classes + code_rows, :2].astype(jnp.int32)
    keep_in = lax.dynamic_index_in_dim(inputs, swapped, 0, keepdims=False)
    give_in = lax.dynamic_index_in_dim(inputs, 1 - swapped, 0, keepdims=False)
    half_pix = PIX // 2
    got_in = [flip(give_in[:, :half_pix], SWAP)]
    got_in.append(flip(after(give_in[:, half_pix:], got_in[0]), SWAP))
    images = 2 * inputs.shape[1]
    rows = images * PIX

    wide_own = wide_weight[0]
    mid_own = mid_weight[0].reshape(-1, narrow)

    def exchange(own, *gate):
        mine = after(split_rows(own, core), *gate)
        return turned(mine, 1, 2), turned(mine, 2, 1)

    def pass_on(own, first, second, *gate):
        pieces = [first, second, turned(after(first, second, *gate), 2, 1)]
        return [own] + pieces + [flip(p, 1) for p in pieces]

    wide = pass_on(wide_own, *exchange(wide_own, give_in), got_in[0], small_x, got_facts)
    mid_two = exchange(mid_own, wide[3])

    local_count = jnp.full((8, 128), jnp.sum(box[:, 0] * box[:, 1]).astype(f32))
    position = jnp.arange(PIX, dtype=jnp.int32)
    inside = (position // FRAME < box[:, 0:1]) & (position % FRAME < box[:, 1:2])
    mask = inside.astype(f32).reshape(rows, 1)

    cot_columns = jnp.pad(cotangent, ((0, 0), (0, HEADS - classes), (0, 0)))
    (merged,) = pl.pallas_call(
        drop_kernel,
        grid=(images,),
        in_specs=[
            pl.BlockSpec((1, 1, channels), lambda i: (i, 0, 0)),
            pl.BlockSpec((1, HEADS, PIX), lambda i: (i, 0, 0)),
            pl.BlockSpec((HEADS, channels), lambda i: (0, 0)),
        ],
        out_specs=[pl.BlockSpec((PIX, channels), lambda i: (i, 0))],
        out_shape=[jax.ShapeDtypeStruct((rows, channels), bf16)],
        compiler_params=pltpu.CompilerParams(vmem_limit_bytes=LIMIT),
    )(codes, cot_columns, head_rows)

    got_in = jnp.concatenate([got_in[0], after(got_in[1], merged)], axis=1)
    entry = jnp.concatenate([keep_in, got_in], axis=0).reshape(rows, channels)

    narrow_f = ((rows, narrow), f32)
    narrow_b = ((rows, narrow), bf16)
    wide_f = ((rows, channels), f32)
    wide_b = ((rows, channels), bf16)
    pair_n = ((2, narrow), f32)
    pair_w = ((2, channels), f32)
    copies_b = ((images, PIX + 2 * PAD, 3 * narrow), bf16)
    w_scratch = [pltpu.VMEM((channels, narrow), bf16), pltpu.SemaphoreType.DMA((4,))]
    m_shape = pltpu.VMEM((9 * half_width, narrow), bf16)
    m_scratch = [m_shape, m_shape, pltpu.SemaphoreType.DMA((4,)), pltpu.SemaphoreType.DMA((4,))]
    w_specs = [ANY] * 7
    product = 2 * rows * channels * narrow
    conv = 2 * rows * 9 * narrow * narrow

    def row(values, k):
        return values[k : k + 1]

    met = {}

    def moments(stats):
        if id(stats) not in met:
            met[id(stats)] = (four_parts(pair_up(stats, local_count)), stats)
        return met[id(stats)][0]

    kept = {}
    z1, st = run(
        functools.partial(first_kernel, 0),
        [place, local_count, entry, mask] + wide,
        [SM, VM, VM, VM] + w_specs,
        [narrow_f, ((8, narrow), f32)],
        w_scratch,
        product,
    )
    mid = pass_on(mid_own, *mid_two, merged, z1)
    group_counts = moments(st)
    number = sum(g[2:3, :128] for g in group_counts)
    group_counts = [g[2:3, :128] for g in group_counts]
    u = entry
    for k in range(2):
        head, tail = 2 * k, 2 * k + 1
        hs, z2, st2, mi1 = run(
            functools.partial(middle_kernel, head),
            [place] + group_counts + [z1] + moments(st) + [row(gain_narrow, head), row(bias_narrow, head), mask] + mid,
            [SM] + [VM] * 12 + w_specs,
            [copies_b, narrow_f, pair_n, pair_n],
            m_scratch,
            conv,
        )
        h2, z3, st3, mi2 = run(
            functools.partial(expand_kernel, tail),
            [place] + group_counts + [z2] + moments(st2) + [row(gain_narrow, tail), row(bias_narrow, tail), mask] + wide,
            [SM] + [VM] * 12 + w_specs,
            [narrow_b, wide_f, pair_w, pair_n],
            w_scratch,
            product,
        )
        kept[k] = dict(z1=z1, mi1=mi1, hs=hs, z2=z2, mi2=mi2, h2=h2, z3=z3, u=u)
        last = [row(gain_wide, k), row(bias_wide, k), u, mask]
        if k == 0:
            u, z1, st, kept[0]["mi3"] = run(
                functools.partial(join_kernel, 2),
                [place] + group_counts + [z3] + moments(st3) + last + wide,
                [SM] + [VM] * 13 + w_specs,
                [wide_b, narrow_f, pair_n, pair_w],
                w_scratch,
                product,
            )
        else:
            ds, n3, sums3, logits, head_grad, mi3 = run(
                turn_kernel,
                group_counts + [z3] + moments(st3) + last + [merged, head_rows, cot_columns],
                [VM] * 16,
                [wide_b, wide_b, pair_w, ((HEADS, rows), f32), ((HEADS, channels), f32), pair_w],
                [pltpu.VMEM((rows, channels // 4), bf16)],
                product // 4,
            )
            kept[1]["mi3"] = mi3

    grads, totals = {}, {}

    def plus(a, b):
        return (a.astype(f32) + b.astype(f32)).astype(bf16)

    def joined(side, mine, other):
        return jnp.where(
            side == 1, jnp.concatenate([other, mine], axis=0), jnp.concatenate([mine, other], axis=0)
        )

    def halves(grad):
        return plus(split_rows(grad, core), flip(split_rows(grad, 1 - core), 1))

    def by_xy(blocks4):
        return [blocks4[i] for i in (0, 2, 1, 3)]

    def quarters(value):
        return jnp.split(value, 4, axis=0)

    z_groups = [[j for j in range(lax.axis_size("dp")) if j % 2 == side] for side in range(2)]

    def slow_xy(blocks4):
        return lax.psum_scatter(jnp.concatenate(by_xy(blocks4), axis=0), "segment", scatter_dimension=0, tiled=True)

    def slow_z(part):
        return lax.psum(part, "dp", axis_index_groups=z_groups)

    first_side, second_side = jnp.where(core == 0, x_side, y_side), jnp.where(core == 0, y_side, x_side)

    def pick(four, start):
        return jnp.stack(
            [lax.dynamic_index_in_dim(four, start + i * (1 + core), 0, keepdims=False) for i in range(2)]
        )

    def quick_sum(blocks4):
        four = jnp.stack(blocks4)
        got = turned(pick(four, (1 - first_side) * (2 - core)), 1, 2)
        yield got
        two = plus(pick(four, first_side * (2 - core)), got)
        got = turned(lax.dynamic_index_in_dim(two, 1 - second_side, 0, keepdims=False), 2, 1)
        yield got
        part = plus(lax.dynamic_index_in_dim(two, second_side, 0, keepdims=False), got)
        bits = dp_bits()[1:]
        for b in bits:
            side = (dp // b) % 2
            part = plus(split_rows(part, side), flip(split_rows(part, 1 - side), b))
        for b in bits[::-1]:
            part = joined((dp // b) % 2, part, flip(part, b))
        return part

    def finish(steps):
        while True:
            try:
                next(steps)
            except StopIteration as end:
                return end.value

    def pair_to_owner(part, k):
        got = lax.ppermute(part, "segment", [(i, i ^ 2) for i in range(sections) if i // 2 != k])
        half = joined(y_side, part, got)
        return joined(core, half, flip(half, 1))

    def tile_grad(left, right, dims=rows_only):
        return lax.dot_general(left, right, dims, preferred_element_type=f32).astype(bf16)

    def conv_grad(hs, dz2, side):
        right = dz2.reshape(images, PIX, narrow)
        both = (((0, 1), (0, 1)), ((), ()))
        width = 3 * half_width
        parts = [
            tile_grad(hs[:, FRAME * d : FRAME * d + PIX, side * width : (side + 1) * width], right, both)
            for d in range(3)
        ]
        return jnp.concatenate(parts, axis=0)

    def sections_of(kind, k):
        pair = [halves(grads[kind, 2 * k + i]) for i in range(2)]
        return [b for v in pair for b in jnp.split(v, 2, axis=0)]

    for k in (1, 0):
        head, tail = 2 * k, 2 * k + 1
        it = kept[k]
        narrow2 = [it["z2"], it["mi2"], row(gain_narrow, tail)]
        narrow1 = [it["z1"], it["mi1"], row(gain_narrow, head)]
        dz3, d2, sums2, totals["wide", k] = run(
            functools.partial(shrink_kernel, tail),
            [place if k else after(place, *four_m1, *four_w1), number, ds, n3] + four_parts(pair_sum(sums3)) + [it["mi3"], row(gain_wide, k), mask]
            + narrow2 + [row(bias_narrow, tail)] + wide,
            [SM] + [VM] * 14 + w_specs,
            [wide_b, narrow_f, pair_n, pair_w],
            w_scratch,
            product,
        )
        grads["w", tail] = tile_grad(dz3, it["h2"])
        hold = place
        if k == 0:
            hold = after(place, w1_step)
            w1_step = next(w1)
        dz2, d1, sums1, totals["narrow", tail] = run(
            functools.partial(unmix_kernel, head),
            [hold, number, d2] + four_parts(pair_sum(sums2)) + narrow2 + [mask] + narrow1
            + [row(bias_narrow, head)] + mid,
            [SM] + [VM] * 14 + w_specs,
            [narrow_b, narrow_f, pair_n, pair_n],
            [pltpu.VMEM(*copies_b)] + m_scratch,
            conv,
        )
        grads["m", head] = conv_grad(it["hs"], dz2, 0)
        grads["m", tail] = conv_grad(it["hs"], dz2, 1)
        if k == 0:
            slow_m1 = slow_xy(four_m1)
            four_m0 = sections_of("m", 0)
            hold = after(place, w1_step, slow_m1, *four_m0)
            slow_m1 = slow_z(slow_m1)
            m0 = quick_sum(four_m0)
        base = [hold, number, d1] + four_parts(pair_sum(sums1)) + narrow1 + [mask, ds]
        if k == 1:
            low = kept[0]
            dz1, ds, n3, sums3, totals["narrow", head] = run(
                functools.partial(widen_kernel, head),
                base + [low["z3"], low["mi3"], row(gain_wide, 0), row(bias_wide, 0), low["u"]] + wide,
                [SM] + [VM] * 16 + w_specs,
                [narrow_b, wide_b, wide_b, pair_w, pair_n],
                [w_scratch[0], pltpu.VMEM((rows, channels // 4), f32), w_scratch[1]],
                product,
            )
            grads["w", head] = tile_grad(it["u"], dz1)
        else:
            dz1, grad_keep, grad_give, totals["narrow", head] = run(
                functools.partial(last_kernel, head),
                base + wide,
                [SM] + [VM] * 11 + w_specs,
                [narrow_b, ((rows // 2, channels), f32), ((rows // 2, channels), bf16), pair_n],
                w_scratch,
                product,
            )
            grads["w", head] = tile_grad(it["u"], dz1)
        if k == 1:
            four_m1 = sections_of("m", 1)
            by_block = head_grad.astype(bf16).reshape(HEADS, 4, narrow).transpose(1, 0, 2)
            extra = halves(by_block.reshape(4, 2, HEADS // 2, narrow).transpose(1, 0, 2, 3).reshape(-1, narrow))
            extra = [quarters(extra)[i] for i in (0, 2, 1, 3)]
            four_w1 = [jnp.concatenate([a, b]) for a, b in zip(sections_of("w", 1), extra)]
            w1 = quick_sum(four_w1)
            w1_step = next(w1)

    w0 = quick_sum(sections_of("w", 0))
    w1, m0, w0 = finish(w1), finish(m0), finish(w0)
    slow_m1 = after(slow_m1, grad_give)
    edge = wide_own.shape[0] // 4
    heads = w1[edge:]
    heads = joined(core, heads, flip(heads, 1))
    mid_grad = jnp.where(y_side == 0, pair_to_owner(m0, 0), pair_to_owner(slow_m1, 1)).astype(f32)
    wide_grad = jnp.where(y_side == 0, pair_to_owner(w0, 0), pair_to_owner(w1[:edge], 1)).astype(f32)

    flat = jnp.concatenate(
        [totals["wide", k].reshape(-1, narrow) for k in range(2)]
        + [totals["narrow", i] for i in range(sections)],
        axis=0,
    )
    flat = flat + flip(flat, SWAP)
    flat = flat + cross(flat, 1)
    flat = flat + cross(flat, 2)
    wide_count = 4 * channels // narrow
    wide_all = flat[:wide_count].reshape(2, 2, channels)
    narrow_all = lax.dynamic_index_in_dim(
        flat[wide_count:].reshape(sections, 2, narrow), seg, 0, keepdims=False
    )
    share = channels // sections
    wide_mine = lax.dynamic_slice_in_dim(wide_all, seg * share, share, 2)

    head_out = heads[:classes].astype(f32).T

    def returned(keep, give):
        got = flip(give, SWAP).astype(f32)
        return jnp.stack([jnp.where(swapped == 0, keep, got), jnp.where(swapped == 0, got, keep)])

    by_image = logits[:classes].reshape(classes, images, PIX).transpose(1, 0, 2)
    logits_out = returned(by_image[: images // 2], by_image[images // 2 :].astype(bf16))
    shape = (images // 2, PIX, channels)
    input_grad = returned(grad_keep.reshape(shape), grad_give.reshape(shape))

    return (
        logits_out,
        input_grad,
        wide_grad[None],
        mid_grad.reshape(1, 9, half_width, narrow),
        narrow_all[1:2],
        narrow_all[0:1],
        wide_mine[:, 1].T,
        wide_mine[:, 0].T,
        head_out,
    )


def solution(mesh):
    return jax.shard_map(
        on_device,
        mesh=mesh,
        in_specs=(
            P("segment", "dp", None, None),
            P(None, "dp", None),
            P("segment", None, None),
            P("segment", None, None, None),
            P("segment", None),
            P("segment", None),
            P("segment", None),
            P("segment", None),
            P("segment", None),
            P(None, "dp", None, None),
            P(None, "dp", None),
        ),
        out_specs=(
            P("segment", "dp", None, None),
            P("segment", "dp", None, None),
            P("segment", None, None),
            P("segment", None, None, None),
            P("segment", None),
            P("segment", None),
            P("segment", None),
            P("segment", None),
            P("segment", None),
        ),
        check_vma=False,
    )
```

```python
import functools

import jax
import jax.numpy as jnp
from jax import lax
from jax.experimental import pallas as pl
from jax.experimental.pallas import tpu as pltpu
from jax.sharding import PartitionSpec as P

KSEG = 40
KDEP = 1
KNOR = 3
FRAME = 16
PIX = FRAME * FRAME
EPS = 1e-05
DROP_FLOOR = 0.01
DROP_SHARPNESS = 8.0
CODE_SCALE = 65536.0
SWAP = 2
STEP = 256
PAD = FRAME
HEADS = 64
LIMIT = 18 << 20
SCALE = 8

f32 = jnp.float32
bf16 = jnp.bfloat16
rows_only = (((0,), (0,)), ((), ()))
last_only = (((1,), (1,)), ((), ()))


def sigmoid(values):
    return 0.5 * jnp.tanh(0.5 * values) + 0.5


def fold(values):
    return jnp.sum(values.reshape(values.shape[0] // 8, 8, values.shape[1]), axis=0)


def over_rows(rows, body, init):
    def one(index, carry):
        return body(pl.ds(pl.multiple_of(index * STEP, STEP), STEP), carry)

    return lax.fori_loop(0, rows // STEP, one, init)


def column_sum(total):
    return jnp.sum(total, axis=0, keepdims=True)


def local_moments(z_ref, cols, mask_ref, count, st_ref, out_ref=None, out_cols=None):
    rows, width = z_ref.shape[0], cols.size
    out_cols = cols if out_cols is None else out_cols
    zero = jnp.zeros((8, width), f32)

    def add(r, total):
        return total + fold(z_ref[r, cols] * mask_ref[r, :])

    total = column_sum(over_rows(rows, add, zero))
    mean = total / count

    def add_square(r, square):
        away = z_ref[r, cols] - mean
        if out_ref is not None:
            out_ref[r, out_cols] = away.astype(bf16)
        return square + fold(away * away * mask_ref[r, :])

    square = column_sum(over_rows(rows, add_square, zero))
    st_ref[0:1, out_cols] = total
    st_ref[1:2, out_cols] = square
    if st_ref.shape[0] > 2:
        st_ref[2:3, out_cols] = jnp.zeros_like(total) + count


def pixels(counts):
    numbers = [c[0:1, 0:1] for c in counts]
    return numbers, (numbers[0] + numbers[1]) + (numbers[2] + numbers[3])


def merged_moments(parts, counts, mi_ref, centered=False):
    numbers, whole = pixels(counts)
    sums = [p[0:1, :] for p in parts]
    squares = [p[1:2, :] for p in parts]
    mean = ((sums[0] + sums[1]) + (sums[2] + sums[3])) / whole
    square = (squares[0] + squares[1]) + (squares[2] + squares[3])
    for s, n in zip(sums, numbers):
        away = s / n - mean
        square = square + away * away * n
    mi_ref[0:1, :] = mean - sums[0] / numbers[0] if centered else mean
    mi_ref[1:2, :] = lax.rsqrt(square / whole + EPS)


def merged_sums(parts, out_ref):
    out_ref[...] = (parts[0][...] + parts[1][...]) + (parts[2][...] + parts[3][...])


class Weights:
    def __init__(self, section, place_ref, sources, buffer, sems):
        self.buffer, self.sems = buffer, sems
        self.piece = buffer.shape[0] // 4
        self.own = own = sources[0]
        first, second, third, other_first, other_second, other_third = sources[1:]
        relative = place_ref[0] ^ section
        core = place_ref[1]
        straight = relative == 1 + core
        near = (relative == 1) | (relative == 2)

        @pl.when(relative == 0)
        def _():
            for i in range(4):
                pltpu.make_async_copy(own.at[pl.ds(i * self.piece, self.piece)], self.part(i), sems.at[i]).start()

        def fetch(mine, other):
            for i in range(4):
                source, side = (mine, core) if i < 2 else (other, 1 - core)
                at = side * 2 + i % 2
                rows = pl.ds(i % 2 * self.piece, self.piece)
                pltpu.make_async_copy(source.at[rows], self.part(at), sems.at[at]).start()

        @pl.when(near & straight)
        def _():
            fetch(first, other_second)

        @pl.when(near & jnp.logical_not(straight))
        def _():
            fetch(second, other_first)

        @pl.when(relative == 3)
        def _():
            fetch(third, other_third)

    def part(self, at):
        start = at * self.piece
        if not isinstance(at, int):
            start = pl.multiple_of(start, 16)
        return self.buffer.at[pl.ds(start, self.piece)]

    def wait(self, at):
        source = self.own.at[pl.ds(0, self.piece)]
        pltpu.make_async_copy(source, self.part(at), self.sems.at[at]).wait()


def blocks(width, count=4):
    size = width // count
    return [pl.ds(i * size, size) for i in range(count)]


def first_kernel(section, place, k0, u, mask, *rest):
    sources, (z, st, w, sems) = rest[:7], rest[7:]
    weights = Weights(section, place, sources, w, sems)
    for i, cols in enumerate(blocks(u.shape[1])):
        weights.wait(i)
        part = jnp.dot(u[:, cols], w[cols, :], preferred_element_type=f32)
        z[...] = part if i == 0 else z[...] + part
    local_moments(z, pl.ds(0, z.shape[1]), mask, k0[0:1, 0:1], st)


def shifted_copies(values, column):
    left = jnp.where(column >= 1, pltpu.roll(values, 1, 0), 0.0)
    right = jnp.where(column < FRAME - 1, pltpu.roll(values, PIX - 1, 0), 0.0)
    return left, values, right


def clear_borders(buffer):
    images, rows, width = buffer.shape
    zero = jnp.zeros((images, PAD, width), bf16)
    buffer[:, 0:PAD, :] = zero
    buffer[:, rows - PAD : rows, :] = zero


def frame_column(width):
    return lax.broadcasted_iota(jnp.int32, (PIX, width), 0) % FRAME


def middle_kernel(section, place, k0, k1, k2, k3, z1, p0, p1, p2, p3, gain, bias, mask, *rest):
    sources, (hs, z2, st, mi, ka, kt, sems_a, sems_t) = rest[:7], rest[7:]
    lower = Weights(section, place, sources, ka, sems_a)
    upper = Weights(section + 1, place, sources, kt, sems_t)
    merged_moments((p0, p1, p2, p3), (k0, k1, k2, k3), mi)
    clear_borders(hs)
    images = hs.shape[0]
    half = z1.shape[1] // 2
    column = frame_column(128)

    def one(image, carry):
        r = pl.ds(pl.multiple_of(image * PIX, PIX), PIX)
        for j in range(z1.shape[1] // 128):
            cols = pl.ds(j * 128, 128)
            n = (z1[r, cols] - mi[0:1, cols]) * mi[1:2, cols]
            a = n * gain[:, cols] + bias[:, cols]
            h = a * sigmoid(a) * mask[r, :]
            side, inner = divmod(j * 128, half)
            for k, copy in enumerate(shifted_copies(h, column)):
                hs[image, PAD : PAD + PIX, pl.ds(side * 3 * half + k * half + inner, 128)] = copy.astype(bf16)
        return carry

    lax.fori_loop(0, images, one, 0)
    for weights in (lower, upper):
        for i in range(4):
            weights.wait(i)
    rows = z1.shape[0]
    for d in range(3):
        taps = hs[:, FRAME * d : FRAME * d + PIX, :].reshape(rows, 6 * half)
        ks = pl.ds(3 * half * d, 3 * half)
        part = jnp.dot(taps[:, : 3 * half], ka[ks, :], preferred_element_type=f32)
        part = part + jnp.dot(taps[:, 3 * half :], kt[ks, :], preferred_element_type=f32)
        z2[...] = part if d == 0 else z2[...] + part
    local_moments(z2, pl.ds(0, z2.shape[1]), mask, k0[0:1, 0:1], st)


def expand_kernel(section, place, k0, k1, k2, k3, z2, p0, p1, p2, p3, gain, bias, mask, *rest):
    sources, (h2, z3, st, mi, w, z, sems) = rest[:7], rest[7:]
    weights = Weights(section, place, sources, w, sems)
    merged_moments((p0, p1, p2, p3), (k0, k1, k2, k3), mi)

    def one(r, carry):
        n = (z2[r, :] - mi[0:1, :]) * mi[1:2, :]
        a = n * gain[...] + bias[...]
        h2[r, :] = (a * sigmoid(a) * mask[r, :]).astype(bf16)
        return carry

    over_rows(z2.shape[0], one, 0)
    for i, cols in enumerate(blocks(z3.shape[1])):
        weights.wait(i)
        z[...] = lax.dot_general(h2[...], w[cols, :], last_only, preferred_element_type=f32)
        local_moments(z, pl.ds(0, z.shape[1]), mask, k0[0:1, 0:1], st, z3, cols)


def join_kernel(section, place, k0, k1, k2, k3, z3, p0, p1, p2, p3, gain, bias, u, mask, *rest):
    sources, (y, z, st, mi, w, sems) = rest[:7], rest[7:]
    weights = Weights(section, place, sources, w, sems)
    merged_moments((p0, p1, p2, p3), (k0, k1, k2, k3), mi, True)
    for i, cols in enumerate(blocks(z3.shape[1])):

        def one(r, carry, cols=cols):
            n = (z3[r, cols].astype(f32) - mi[0:1, cols]) * mi[1:2, cols]
            s = n * gain[:, cols] + bias[:, cols] + u[r, cols].astype(f32)
            y[r, cols] = (s * sigmoid(s) * mask[r, :]).astype(bf16)
            return carry

        over_rows(z3.shape[0], one, 0)
        weights.wait(i)
        part = jnp.dot(y[:, cols], w[cols, :], preferred_element_type=f32)
        z[...] = part if i == 0 else z[...] + part
    local_moments(z, pl.ds(0, z.shape[1]), mask, k0[0:1, 0:1], st)


def slope_of(s):
    part = sigmoid(s)
    return part, part * (1.0 + s * (1.0 - part))


def turn_kernel(k0, k1, k2, k3, z3, p0, p1, p2, p3, gain, bias, u, mask, merged, head, cot, ds, sums, logits, hgrad, mi, y):
    merged_moments((p0, p1, p2, p3), (k0, k1, k2, k3), mi, True)
    for i, cols in enumerate(blocks(z3.shape[1])):
        width = cols.size

        def one(r, carry, cols=cols):
            n = (z3[r, cols].astype(f32) - mi[0:1, cols]) * mi[1:2, cols]
            s = n * gain[:, cols] + bias[:, cols] + u[r, cols].astype(f32)
            part, slope = slope_of(s)
            y[r, :] = (s * part * mask[r, :]).astype(bf16)
            d = merged[r, cols].astype(f32) * mask[r, :] * slope
            ds[r, cols] = d.astype(bf16)
            return carry[0] + fold(d), carry[1] + fold(d * n)

        zero = jnp.zeros((8, width), f32)
        both = over_rows(z3.shape[0], one, (zero, zero))
        sums[0:1, cols] = column_sum(both[0])
        sums[1:2, cols] = column_sum(both[1])
        part = lax.dot_general(head[:, cols], y[...], last_only, preferred_element_type=f32)
        logits[...] = part if i == 0 else logits[...] + part
        for image in range(cot.shape[0]):
            r = pl.ds(image * PIX, PIX)
            part = jnp.dot(cot[image], y[r, :], preferred_element_type=f32)
            grad = part if image == 0 else grad + part
        for side in range(2):
            size = grad.shape[0] // 2
            hgrad[side, i % 2 * 2 + i // 2] = grad[side * size : (side + 1) * size].astype(bf16)


def shrink_kernel(place, number, ds, z3, q0, q1, q2, q3, mi3, gain3, mask, z2, mi2, gain2, bias2, w, dz3, d2, sums, tot):
    merged_sums((q0, q1, q2, q3), tot)
    for i, cols in enumerate(blocks(ds.shape[1])):
        g = gain3[:, cols] * mi3[1:2, cols]
        c1 = g * tot[0:1, cols] / number[0:1, 0:1]
        c2 = g * tot[1:2, cols] / number[0:1, 0:1]

        def one(r, carry, cols=cols, g=g, c1=c1, c2=c2):
            n = (z3[r, cols].astype(f32) - mi3[0:1, cols]) * mi3[1:2, cols]
            d = g * ds[r, cols].astype(f32) - (c1 + n * c2)
            dz3[r, cols] = (mask[r, :] * d).astype(bf16)
            return carry

        over_rows(ds.shape[0], one, 0)
        part = jnp.dot(dz3[:, cols], w[cols, :], preferred_element_type=f32)
        d2[...] = part if i == 0 else d2[...] + part
    narrow_back(d2, z2, mi2, gain2, bias2, mask, sums)


def narrow_back(d, z, mi, gain, bias, mask, sums):
    zero = jnp.zeros((8, z.shape[1]), f32)

    def one(r, carry):
        n = (z[r, :] - mi[0:1, :]) * mi[1:2, :]
        slope = slope_of(n * gain[...] + bias[...])[1]
        value = d[r, :] * mask[r, :] * slope
        d[r, :] = value
        return carry[0] + fold(value), carry[1] + fold(value * n)

    both = over_rows(z.shape[0], one, (zero, zero))
    sums[0:1, :] = column_sum(both[0])
    sums[1:2, :] = column_sum(both[1])


def unmix_kernel(place, number, d2, q0, q1, q2, q3, z2, mi2, gain2, mask, z1, mi1, gain1, bias1, ka, kt, dz2, d1, sums, tot, gs):
    merged_sums((q0, q1, q2, q3), tot)
    clear_borders(gs)
    images = gs.shape[0]
    rows, width = z2.shape
    half = width // 2
    column = frame_column(128)

    def one(image, carry):
        r = pl.ds(pl.multiple_of(image * PIX, PIX), PIX)
        for j in range(width // 128):
            cols = pl.ds(j * 128, 128)
            g = gain2[:, cols] * mi2[1:2, cols]
            c1 = g * tot[0:1, cols] / number[0:1, 0:1]
            c2 = g * tot[1:2, cols] / number[0:1, 0:1]
            n = (z2[r, cols] - mi2[0:1, cols]) * mi2[1:2, cols]
            d = mask[r, :] * (g * d2[r, cols] - (c1 + n * c2))
            dz2[r, cols] = d.astype(bf16)
            for k, copy in enumerate(shifted_copies(d, column)):
                gs[image, PAD : PAD + PIX, pl.ds(k * width + j * 128, 128)] = copy.astype(bf16)
        return carry

    lax.fori_loop(0, images, one, 0)
    for d in range(3):
        for k in range(3):
            moved = gs[:, FRAME * (2 - d) : FRAME * (2 - d) + PIX, pl.ds((2 - k) * width, width)]
            moved = moved.reshape(rows, width)
            tap = pl.ds((3 * d + k) * half, half)
            for side, kernel in enumerate((ka, kt)):
                cols = pl.ds(side * half, half)
                part = lax.dot_general(moved, kernel[tap, :], last_only, preferred_element_type=f32)
                d1[:, cols] = part if d + k == 0 else d1[:, cols] + part
    narrow_back(d1, z1, mi1, gain1, bias1, mask, sums)


def narrow_finish(d1, q, z1, mi1, gain1, mask, number, dz1, tot):
    merged_sums(q, tot)
    g = gain1[...] * mi1[1:2, :]
    c1 = g * tot[0:1, :] / number[0:1, 0:1]
    c2 = g * tot[1:2, :] / number[0:1, 0:1]

    def one(r, carry):
        n = (z1[r, :] - mi1[0:1, :]) * mi1[1:2, :]
        dz1[r, :] = (mask[r, :] * (g * d1[r, :] - (c1 + n * c2))).astype(bf16)
        return carry

    over_rows(z1.shape[0], one, 0)


def widen_kernel(place, number, d1, q0, q1, q2, q3, z1, mi1, gain1, mask, ds, z3, mi3, gain3, bias3, u, w, dz1, ds0, sums, tot, du):
    narrow_finish(d1, (q0, q1, q2, q3), z1, mi1, gain1, mask, number, dz1, tot)
    for i, cols in enumerate(blocks(ds.shape[1])):
        du[...] = lax.dot_general(dz1[...], w[cols, :], last_only, preferred_element_type=f32)

        def one(r, carry, cols=cols):
            dy = (du[r, :] + ds[r, cols].astype(f32)).astype(bf16).astype(f32)
            n = (z3[r, cols].astype(f32) - mi3[0:1, cols]) * mi3[1:2, cols]
            s = n * gain3[:, cols] + bias3[:, cols] + u[r, cols].astype(f32)
            d = dy * mask[r, :] * slope_of(s)[1]
            ds0[r, cols] = d.astype(bf16)
            return carry[0] + fold(d), carry[1] + fold(d * n)

        zero = jnp.zeros((8, cols.size), f32)
        both = over_rows(ds.shape[0], one, (zero, zero))
        sums[0:1, cols] = column_sum(both[0])
        sums[1:2, cols] = column_sum(both[1])


def last_kernel(place, number, d1, q0, q1, q2, q3, z1, mi1, gain1, mask, ds, w, dz1, keep, give, tot):
    narrow_finish(d1, (q0, q1, q2, q3), z1, mi1, gain1, mask, number, dz1, tot)
    half = keep.shape[0]
    for i, cols in enumerate(blocks(ds.shape[1])):
        block = lax.dot_general(dz1[...], w[cols, :], last_only, preferred_element_type=f32)
        keep[:, cols] = block[:half] + ds[:half, cols].astype(f32)
        give[:, cols] = (block[half:] + ds[half:, cols].astype(f32)).astype(bf16)


def in_place_kernel(where, mine, other, out):
    core, y_side = where[0], where[2]
    size = mine.shape[0] // 2
    for source, side in ((mine, core), (other, 1 - core)):
        for y in range(2):
            at = pl.multiple_of((side * 2 + (y ^ y_side)) * size, 16)
            out[pl.ds(at, size), :] = source[pl.ds(y * size, size), :].astype(f32)


def first_mix_kernel(shares, where, *refs):
    give, keep = refs[-2:]
    core, x_side, y_side = where[0], where[1], where[2]
    for section in range(2):
        for half in range(2):
            kept = jnp.where(core == 0, section == x_side, half == y_side)
            at = jnp.where(core == 0, half, section)
            for out, chosen in ((keep, kept), (give, jnp.logical_not(kept))):

                @pl.when(chosen)
                def _(out=out, at=at, section=section, half=half):
                    start = 0
                    for k, share in enumerate(shares):
                        own, other = refs[4 * k + 2 * section : 4 * k + 2 * section + 2]
                        rows = pl.ds(half * share, share)
                        value = own[rows, :].astype(f32) + other[rows, :].astype(f32)
                        out[at, pl.ds(start, share), :] = value.astype(bf16)
                        start += share


def second_mix_kernel(where, keep, got, give_out, keep_out):
    for at in range(2):
        for out, chosen in ((keep_out, at == where[0]), (give_out, at != where[0])):

            @pl.when(chosen)
            def _(out=out):
                out[...] = (keep[at].astype(f32) + got[at].astype(f32)).astype(bf16)


def drop_kernel(codes, cots, head, merged):
    line = lax.broadcasted_iota(jnp.int32, cots.shape[1:], 0)
    bounds = (0, KSEG, KSEG + KDEP, KSEG + KDEP + KNOR)
    cot = cots[0].astype(f32)
    tasks = [
        jnp.where((line >= a) & (line < b), cot, 0.0).T.astype(bf16)
        for a, b in zip(bounds[:-1], bounds[1:])
    ]
    for cols in blocks(head.shape[1], 8):
        g = [jnp.dot(task, head[:, cols], preferred_element_type=f32) for task in tasks]
        total = g[0] + g[1] + g[2]
        magnitude = sum(jnp.sqrt(v * v + DROP_FLOOR * DROP_FLOOR) for v in g)
        purity = 0.5 + 0.5 * (total / magnitude)
        bar = (codes[0, :, cols] + 0.5) / CODE_SCALE
        keep = sigmoid((purity - bar) * DROP_SHARPNESS)
        lose = 1.0 - keep
        value = sum(v * jnp.where(v > 0.0, keep, lose) for v in g)
        merged[:, cols] = value.astype(bf16)


VM = pl.BlockSpec(memory_space=pltpu.VMEM)
SM = pl.BlockSpec(memory_space=pltpu.SMEM)
ANY = pl.BlockSpec(memory_space=pltpu.HBM)


def run(kernel, operands, specs, outs, scratch, flops):
    return pl.pallas_call(
        kernel,
        out_shape=[jax.ShapeDtypeStruct(shape, kind) for shape, kind in outs],
        in_specs=specs,
        out_specs=[VM] * len(outs),
        scratch_shapes=scratch,
        compiler_params=pltpu.CompilerParams(vmem_limit_bytes=LIMIT),
        cost_estimate=pl.CostEstimate(
            flops=SCALE * flops,
            bytes_accessed=SCALE * sum(o.size * o.dtype.itemsize for o in operands[:16]),
            transcendentals=0,
        ),
    )(*operands)


def flip(value, bits):
    count = lax.axis_size("dp")
    return lax.ppermute(value, "dp", [(i, i ^ bits) for i in range(count)])


def cross(value, bits):
    count = lax.axis_size("segment")
    return lax.ppermute(value, "segment", [(i, i ^ bits) for i in range(count)])


def turned(value, even, odd):
    size, count = lax.axis_size("segment"), lax.axis_size("dp")
    pairs = [
        (i * count + j, (i ^ (odd if j % 2 else even)) * count + j) for i in range(size) for j in range(count)
    ]
    return lax.ppermute(value, ("segment", "dp"), pairs)


def after(value, *others):
    return lax.optimization_barrier((value,) + others)[0]


def dp_bits():
    count = lax.axis_size("dp")
    return [1 << k for k in range(count.bit_length() - 1)]


def group_bits():
    bits = [b for b in dp_bits() if b != SWAP]
    return bits[:2], bits[2:]


def four_parts(value):
    first, _ = group_bits()
    near = jnp.stack([value, flip(value, first[0])])
    far = flip(near, first[1])
    return [near[0], near[1], far[0], far[1]]


def pair_up(stats, count):
    for b in group_bits()[1]:
        other, other_count = flip(stats, b), flip(count, b)
        whole = count + other_count
        here, there = count[0, 0], other_count[0, 0]
        away = stats[0] / here - other[0] / there
        square = stats[1] + other[1] + away * away * (here * there / (here + there))
        merged = jnp.stack([stats[0] + other[0], square])
        if stats.shape[0] > 2:
            merged = jnp.concatenate([merged, stats[2:] + other[2:]], axis=0)
        stats, count = merged, whole
    return stats


def pair_sum(value):
    for b in group_bits()[1]:
        value = value + flip(value, b)
    return value


def split_rows(value, index, parts=2):
    size = value.shape[0] // parts
    return lax.dynamic_slice_in_dim(value, index * size, size, 0)


def on_device(
    inputs,
    extents,
    wide_weight,
    mid_weight,
    narrow_gain,
    narrow_bias,
    expand_gain,
    expand_bias,
    head_weight,
    head_cotangent,
    drop_codes,
):
    seg = lax.axis_index("segment")
    dp = lax.axis_index("dp")
    sections = lax.axis_size("segment")
    x_side, y_side, core = seg % 2, seg // 2, dp % 2
    swapped = (dp // SWAP) % 2
    channels = inputs.shape[-1]
    narrow = wide_weight.shape[-1]
    half_width = narrow // 2
    classes = head_weight.shape[-1]
    place = jnp.stack([seg, core]).astype(jnp.int32)

    own_small = jnp.concatenate(
        [head_weight.T, jnp.zeros((HEADS - classes, head_weight.shape[0]), bf16), expand_gain.T, expand_bias.T]
        + [narrow_gain, narrow_bias, jnp.zeros((10, narrow), bf16)],
        axis=0,
    )
    small_x = cross(own_small, 1)
    small_y = cross(jnp.stack([own_small, small_x]), 2)
    small = jnp.stack([own_small, small_x, small_y[0], small_y[1]])
    small = jnp.stack([lax.dynamic_index_in_dim(small, k ^ seg, 0, keepdims=False) for k in range(4)])
    lanes = jnp.moveaxis(small[:, : HEADS + 4], 0, 1).reshape(HEADS + 4, channels)
    head_rows = lanes[:HEADS]
    gain_wide = lanes[HEADS : HEADS + 2].astype(f32)
    bias_wide = lanes[HEADS + 2 : HEADS + 4].astype(f32)
    gain_narrow = small[:, HEADS + 4].astype(f32)
    bias_narrow = small[:, HEADS + 5].astype(f32)

    own_count = inputs.shape[0]
    start = seg * own_count

    def own_part(value):
        return lax.dynamic_slice_in_dim(value, start, own_count, 0).astype(f32).reshape(own_count, -1, PIX)

    boxes = jnp.pad(extents, ((0, 0), (0, 0), (0, PIX - 2)))
    facts = jnp.concatenate([own_part(v) for v in (head_cotangent, drop_codes, boxes)], axis=1)
    facts = jnp.pad(facts, ((0, 0), (0, -facts.shape[1] % 8), (0, 0)))
    keep_facts = lax.dynamic_index_in_dim(facts, swapped, 0, keepdims=False)
    got_facts = flip(lax.dynamic_index_in_dim(facts, 1 - swapped, 0, keepdims=False), SWAP)
    facts = jnp.stack([keep_facts, got_facts])
    code_rows = channels // PIX
    cotangent = facts[:, :classes].astype(bf16)
    codes = facts[:, classes : classes + code_rows].reshape(2, 1, channels)
    box = facts[:, classes + code_rows, :2].astype(jnp.int32)
    keep_in = lax.dynamic_index_in_dim(inputs, swapped, 0, keepdims=False)
    give_in = lax.dynamic_index_in_dim(inputs, 1 - swapped, 0, keepdims=False)
    half_pix = PIX // 2
    got_in = [flip(give_in[:, :half_pix], SWAP)]
    got_in.append(flip(after(give_in[:, half_pix:], got_in[0]), SWAP))
    images = 2 * inputs.shape[1]
    rows = images * PIX

    wide_own = wide_weight[0]
    mid_own = mid_weight[0].reshape(-1, narrow)

    def exchange(own, *gate):
        mine = after(split_rows(own, core), *gate)
        return turned(mine, 1, 2), turned(mine, 2, 1)

    def pass_on(own, first, second, *gate):
        pieces = [first, second, turned(after(first, second, *gate), 2, 1)]
        return [own] + pieces + [flip(p, 1) for p in pieces]

    wide = pass_on(wide_own, *exchange(wide_own, give_in), got_in[0], small_x, got_facts)
    mid_two = exchange(mid_own, wide[1], wide[2])

    local_count = jnp.full((8, 128), jnp.sum(box[:, 0] * box[:, 1]).astype(f32))
    position = jnp.arange(PIX, dtype=jnp.int32)
    inside = (position // FRAME < box[:, 0:1]) & (position % FRAME < box[:, 1:2])
    mask = inside.astype(f32).reshape(rows, 1)

    cot_columns = jnp.pad(cotangent, ((0, 0), (0, HEADS - classes), (0, 0)))
    (merged,) = pl.pallas_call(
        drop_kernel,
        grid=(images,),
        in_specs=[
            pl.BlockSpec((1, 1, channels), lambda i: (i, 0, 0)),
            pl.BlockSpec((1, HEADS, PIX), lambda i: (i, 0, 0)),
            pl.BlockSpec((HEADS, channels), lambda i: (0, 0)),
        ],
        out_specs=[pl.BlockSpec((PIX, channels), lambda i: (i, 0))],
        out_shape=[jax.ShapeDtypeStruct((rows, channels), bf16)],
        compiler_params=pltpu.CompilerParams(vmem_limit_bytes=LIMIT),
    )(codes, cot_columns, head_rows)

    got_in = jnp.concatenate([got_in[0], after(got_in[1], merged)], axis=1)
    entry = jnp.concatenate([keep_in, got_in], axis=0).reshape(rows, channels)

    narrow_f = ((rows, narrow), f32)
    narrow_b = ((rows, narrow), bf16)
    wide_f = ((rows, channels), f32)
    wide_b = ((rows, channels), bf16)
    pair_n = ((2, narrow), f32)
    pair_w = ((2, channels), f32)
    copies_b = ((images, PIX + 2 * PAD, 3 * narrow), bf16)
    w_out = ((channels, narrow), bf16)
    m_out = ((9 * half_width, narrow), bf16)
    w_scratch = [None, pltpu.SemaphoreType.DMA((4,))]
    m_scratch = [pltpu.SemaphoreType.DMA((4,)), pltpu.SemaphoreType.DMA((4,))]
    w_specs = [ANY] * 7
    product = 2 * rows * channels * narrow
    conv = 2 * rows * 9 * narrow * narrow

    def row(values, k):
        return values[k : k + 1]

    met = {}

    def moments(stats):
        if id(stats) not in met:
            met[id(stats)] = (four_parts(pair_up(stats, local_count)), stats)
        return met[id(stats)][0]

    kept = {}
    z1, st, w_head = run(
        functools.partial(first_kernel, 0),
        [place, local_count, entry, mask] + wide,
        [SM, VM, VM, VM] + w_specs,
        [narrow_f, ((8, narrow), f32), w_out],
        w_scratch[1:],
        product,
    )
    mid = pass_on(mid_own, *mid_two, merged, z1)
    group_counts = moments(st)
    number = sum(g[2:3, :128] for g in group_counts)
    group_counts = [g[2:3, :128] for g in group_counts]
    u = entry
    for k in range(2):
        head, tail = 2 * k, 2 * k + 1
        hs, z2, st2, mi1, ka, kt = run(
            functools.partial(middle_kernel, head),
            [place] + group_counts + [z1] + moments(st) + [row(gain_narrow, head), row(bias_narrow, head), mask] + mid,
            [SM] + [VM] * 12 + w_specs,
            [copies_b, narrow_f, pair_n, pair_n, m_out, m_out],
            m_scratch,
            conv,
        )
        h2, z3, st3, mi2, w_tail = run(
            functools.partial(expand_kernel, tail),
            [place] + group_counts + [z2] + moments(st2) + [row(gain_narrow, tail), row(bias_narrow, tail), mask] + wide,
            [SM] + [VM] * 12 + w_specs,
            [narrow_b, wide_b, pair_w, pair_n, w_out],
            [pltpu.VMEM((rows, channels // 4), f32), w_scratch[1]],
            product,
        )
        kept[k] = dict(z1=z1, mi1=mi1, hs=hs, z2=z2, mi2=mi2, h2=h2, z3=z3, u=u, ka=ka, kt=kt, w_head=w_head, w_tail=w_tail)
        last = [row(gain_wide, k), row(bias_wide, k), u, mask]
        if k == 0:
            u, z1, st, kept[0]["mi3"], w_head = run(
                functools.partial(join_kernel, 2),
                [place] + group_counts + [z3] + moments(st3) + last + wide,
                [SM] + [VM] * 13 + w_specs,
                [wide_b, narrow_f, pair_n, pair_w, w_out],
                w_scratch[1:],
                product,
            )
        else:
            ds, sums3, logits, head_grad, mi3 = run(
                turn_kernel,
                group_counts + [z3] + moments(st3) + last + [merged, head_rows, cot_columns],
                [VM] * 16,
                [wide_b, pair_w, ((HEADS, rows), f32), ((2, 4, HEADS // 2, channels // 4), bf16), pair_w],
                [pltpu.VMEM((rows, channels // 4), bf16)],
                product // 4,
            )
            kept[1]["mi3"] = mi3

    grads, totals = {}, {}

    def plus(a, b):
        return (a.astype(f32) + b.astype(f32)).astype(bf16)

    def joined(side, mine, other):
        return jnp.where(
            side == 1, jnp.concatenate([other, mine], axis=0), jnp.concatenate([mine, other], axis=0)
        )

    second_side = jnp.where(core == 0, y_side, x_side).astype(jnp.int32)
    sides = jnp.stack([core, x_side, y_side]).astype(jnp.int32)

    class Chain:
        def __init__(self, kinds):
            shares = tuple(kind[0].shape[0] // 2 for kind in kinds)
            shape = jax.ShapeDtypeStruct((2, sum(shares), narrow), bf16)
            operands = [value for kind in kinds for value in kind]
            self.give, self.keep = pl.pallas_call(
                functools.partial(first_mix_kernel, shares),
                in_specs=[SM] + [VM] * len(operands),
                out_specs=[VM, VM],
                out_shape=[shape, shape],
                compiler_params=pltpu.CompilerParams(vmem_limit_bytes=LIMIT),
            )(sides, *operands)
            self.todo = ["first", "second"]
            self.todo += ["in", "mid", "out"] if z_chips == 4 else [("meet", b) for b in dp_bits()[1:]]

        def send(self):
            step = self.todo.pop(0)
            if step == "first":
                self.got = turned(self.give, 1, 2)
            elif step == "second":
                self.got = turned(self.give, 2, 1)
            elif isinstance(step, tuple):
                self.got = flip(self.part, step[1])
            else:
                ways = {"in": [(0, 1), (3, 2)], "mid": [(1, 2), (2, 1)], "out": [(1, 0), (2, 3)]}[step]
                self.got = lax.ppermute(
                    self.part, "dp", [(2 * a + c, 2 * b + c) for a, b in ways for c in range(2)]
                )
            self.step = step
            return self.got

        def take(self, *holds):
            got = after(self.got, *holds)
            if self.todo[:1] == ["second"]:
                shape = jax.ShapeDtypeStruct(got.shape[1:], bf16)
                self.give, self.keep = pl.pallas_call(
                    second_mix_kernel,
                    in_specs=[SM, VM, VM],
                    out_specs=[VM, VM],
                    out_shape=[shape, shape],
                    compiler_params=pltpu.CompilerParams(vmem_limit_bytes=LIMIT),
                )(second_side.reshape(1), self.keep, got)
                return self.give
            if self.step == "second":
                self.part = plus(self.keep, got)
            elif self.step == "out":
                self.part = jnp.where((z_place == 1) | (z_place == 2), self.part, got)
            else:
                self.part = plus(self.part, got)
            return self.part

    z_chips = lax.axis_size("dp") // 2
    z_place = dp // 2

    def to_owner(part, part1):
        keep = jnp.where(y_side == 0, part, part1)
        return jnp.concatenate([keep, cross(jnp.where(y_side == 0, part1, part), 2)])

    def in_place(half):
        (out,) = pl.pallas_call(
            in_place_kernel,
            in_specs=[SM, VM, VM],
            out_specs=[VM],
            out_shape=[jax.ShapeDtypeStruct((2 * half.shape[0], narrow), f32)],
            compiler_params=pltpu.CompilerParams(vmem_limit_bytes=LIMIT),
        )(sides, half, flip(half, 1))
        return out

    def tile_grad(left, right, dims=rows_only):
        return lax.dot_general(left, right, dims, preferred_element_type=f32).astype(bf16)

    def conv_grad(hs, dz2, side):
        right = dz2.reshape(images, PIX, narrow)
        both = (((0, 1), (0, 1)), ((), ()))
        width = 3 * half_width
        parts = [
            tile_grad(hs[:, FRAME * d : FRAME * d + PIX, side * width : (side + 1) * width], right, both)
            for d in range(3)
        ]
        whole = jnp.concatenate(parts, axis=0)
        return split_rows(whole, core), flip(split_rows(whole, 1 - core), 1)

    def sections_of(kind, k):
        return [v for i in range(2) for v in grads[kind, 2 * k + i]]

    def split_grad(left, right):
        size = left.shape[1] // 2
        mine, other = [tile_grad(lax.dynamic_slice_in_dim(left, c * size, size, 1), right) for c in (core, 1 - core)]
        return mine, flip(other, 1)

    for k in (1, 0):
        head, tail = 2 * k, 2 * k + 1
        it = kept[k]
        narrow2 = [it["z2"], it["mi2"], row(gain_narrow, tail)]
        narrow1 = [it["z1"], it["mi1"], row(gain_narrow, head)]
        dz3, d2, sums2, totals["wide", k] = run(
            shrink_kernel,
            [place if k else first_hold, number, ds, it["z3"]] + four_parts(pair_sum(sums3)) + [it["mi3"], row(gain_wide, k), mask]
            + narrow2 + [row(bias_narrow, tail), it["w_tail"]],
            [SM] + [VM] * 15,
            [wide_b, narrow_f, pair_n, pair_w],
            [],
            product,
        )
        grads["w", tail] = split_grad(dz3, it["h2"])
        parts2 = four_parts(pair_sum(sums2))
        hold = place
        if k == 0:
            hold = after(place, m1.take(), w1.take(m1.part))
            w1.send()
        dz2, d1, sums1, totals["narrow", tail] = run(
            unmix_kernel,
            [hold, number, d2] + parts2 + narrow2 + [mask] + narrow1
            + [row(bias_narrow, head), it["ka"], it["kt"]],
            [SM] + [VM] * 16,
            [narrow_b, narrow_f, pair_n, pair_n],
            [pltpu.VMEM(*copies_b)],
            conv,
        )
        parts1 = four_parts(pair_sum(sums1))
        grads["m", head] = conv_grad(it["hs"], dz2, 0)
        grads["m", tail] = conv_grad(it["hs"], dz2, 1)
        hold = place
        if k == 1:
            m1 = Chain([sections_of("m", 1)])
            m1.send()
            hold = after(place, m1.give)
        else:
            m1.part = after(m1.part, *parts1)
            m1.send()
            m0 = Chain([sections_of("m", 0)])
            hold = after(place, w1.take(), m0.give)
            m0.send()
        base = [hold, number, d1] + parts1 + narrow1 + [mask, ds]
        if k == 1:
            low = kept[0]
            dz1, ds, sums3, totals["narrow", head] = run(
                widen_kernel,
                base + [low["z3"], low["mi3"], row(gain_wide, 0), row(bias_wide, 0), low["u"], it["w_head"]],
                [SM] + [VM] * 17,
                [narrow_b, wide_b, pair_w, pair_n],
                [pltpu.VMEM((rows, channels // 4), f32)],
                product,
            )
            grads["w", head] = split_grad(it["u"], dz1)
        else:
            dz1, grad_keep, grad_give, totals["narrow", head] = run(
                last_kernel,
                base + [it["w_head"]],
                [SM] + [VM] * 12,
                [narrow_b, ((rows // 2, channels), f32), ((rows // 2, channels), bf16), pair_n],
                [],
                product,
            )
            grads["w", head] = split_grad(it["u"], dz1)
        if k == 1:
            own = lax.dynamic_index_in_dim(head_grad, core, 0, keepdims=False)
            other = flip(lax.dynamic_index_in_dim(head_grad, 1 - core, 0, keepdims=False), 1)
            extra = [v[2 * i : 2 * i + 2].reshape(-1, narrow) for i in range(2) for v in (own, other)]
            w1 = Chain([sections_of("w", 1), extra])
            w1.send()
            first_hold = after(place, w1.give, m1.take())
            m1.send()
    flat = jnp.concatenate(
        [totals["wide", k].reshape(-1, narrow) for k in range(2)]
        + [totals["narrow", i] for i in range(sections)],
        axis=0,
    )
    def returned(keep, got):
        got = got.astype(f32)
        return jnp.stack([jnp.where(swapped == 0, keep, got), jnp.where(swapped == 0, got, keep)])

    home = flip(grad_give, SWAP)
    w0 = Chain([sections_of("w", 0)])
    w0.send()
    tick = m0.take(w0.give)
    m0.send()
    tick = m1.take(tick)
    m1.send()
    w1.part = after(w1.part, tick)
    w1.send()
    tick = m0.take(tick)
    m0.send()
    tick = w0.take(tick)
    w0.send()
    shape = (images // 2, PIX, channels)
    input_grad = returned(grad_keep.reshape(shape), after(home, tick).reshape(shape))
    tick = m1.take(tick, home)
    m1.send()
    tick = w0.take(tick)
    w0.send()
    flat = flat + cross(flat, 1)
    tick = w1.take(tick)
    w1.send()
    tick = m0.take(tick, input_grad, flat)
    m0.send()
    flat = flat + cross(flat, 2)
    by_image = after(logits, tick)[:classes].reshape(classes, images, PIX).transpose(1, 0, 2)
    logits_out = returned(by_image[: images // 2], flip(by_image[images // 2 :].astype(bf16), SWAP))
    tick = m1.take(tick)
    tick = w1.take(tick)
    w1.send()
    tick = w0.take(tick, flat)
    w0.send()
    flat = flat + flip(flat, SWAP)
    tick = m0.take(tick, logits_out)
    m0.send()
    tick = w1.take(tick)
    edge = wide_own.shape[0] // 4
    heads = joined(core, w1.part[edge:], flip(w1.part[edge:], 1))
    tick = w0.take(tick)
    w0.send()
    tick = m0.take(tick, flat, heads)
    mid_half = to_owner(m0.part, m1.part)
    wide_half = to_owner(w0.take(tick), w1.part[:edge])
    mid_grad = in_place(mid_half)
    wide_grad = in_place(wide_half)

    wide_count = 4 * channels // narrow
    wide_all = flat[:wide_count].reshape(2, 2, channels)
    narrow_all = lax.dynamic_index_in_dim(
        flat[wide_count:].reshape(sections, 2, narrow), seg, 0, keepdims=False
    )
    share = channels // sections
    wide_mine = lax.dynamic_slice_in_dim(wide_all, seg * share, share, 2)

    head_out = heads[:classes].astype(f32).T

    return (
        logits_out,
        input_grad,
        wide_grad[None],
        mid_grad.reshape(1, 9, half_width, narrow),
        narrow_all[1:2],
        narrow_all[0:1],
        wide_mine[:, 1].T,
        wide_mine[:, 0].T,
        head_out,
    )


def solution(mesh):
    return jax.shard_map(
        on_device,
        mesh=mesh,
        in_specs=(
            P("segment", "dp", None, None),
            P(None, "dp", None),
            P("segment", None, None),
            P("segment", None, None, None),
            P("segment", None),
            P("segment", None),
            P("segment", None),
            P("segment", None),
            P("segment", None),
            P(None, "dp", None, None),
            P(None, "dp", None),
        ),
        out_specs=(
            P("segment", "dp", None, None),
            P("segment", "dp", None, None),
            P("segment", None, None),
            P("segment", None, None, None),
            P("segment", None),
            P("segment", None),
            P("segment", None),
            P("segment", None),
            P("segment", None),
        ),
        check_vma=False,
    )
```

```python
import functools

import jax
import jax.numpy as jnp
from jax import lax
from jax.experimental import pallas as pl
from jax.experimental.pallas import tpu as pltpu
from jax.sharding import PartitionSpec as P

KSEG = 40
KDEP = 1
KNOR = 3
FRAME = 16
PIX = FRAME * FRAME
EPS = 1e-05
DROP_FLOOR = 0.01
DROP_SHARPNESS = 8.0
CODE_SCALE = 65536.0
SWAP = 2
STEP = 256
PAD = FRAME
HEADS = 64
LIMIT = 18 << 20
SCALE = 8

f32 = jnp.float32
bf16 = jnp.bfloat16
rows_only = (((0,), (0,)), ((), ()))
last_only = (((1,), (1,)), ((), ()))


def sigmoid(values):
    return 0.5 * jnp.tanh(0.5 * values) + 0.5


def fold(values):
    return jnp.sum(values.reshape(values.shape[0] // 8, 8, values.shape[1]), axis=0)


def over_rows(rows, body, init):
    def one(index, carry):
        return body(pl.ds(pl.multiple_of(index * STEP, STEP), STEP), carry)

    return lax.fori_loop(0, rows // STEP, one, init)


def column_sum(total):
    return jnp.sum(total, axis=0, keepdims=True)


def local_moments(z_ref, cols, mask_ref, count, st_ref, out_ref=None, out_cols=None):
    rows, width = z_ref.shape[0], cols.size
    out_cols = cols if out_cols is None else out_cols
    zero = jnp.zeros((8, width), f32)

    def add(r, total):
        return total + fold(z_ref[r, cols] * mask_ref[r, :])

    total = column_sum(over_rows(rows, add, zero))
    mean = total / count

    def add_square(r, square):
        away = z_ref[r, cols] - mean
        if out_ref is not None:
            out_ref[r, out_cols] = away.astype(bf16)
        return square + fold(away * away * mask_ref[r, :])

    square = column_sum(over_rows(rows, add_square, zero))
    st_ref[0:1, out_cols] = total
    st_ref[1:2, out_cols] = square
    if st_ref.shape[0] > 2:
        st_ref[2:3, out_cols] = jnp.zeros_like(total) + count


def pixels(counts):
    numbers = [c[0:1, 0:1] for c in counts]
    return numbers, (numbers[0] + numbers[1]) + (numbers[2] + numbers[3])


def merged_moments(parts, counts, mi_ref, centered=False):
    numbers, whole = pixels(counts)
    sums = [p[0:1, :] for p in parts]
    squares = [p[1:2, :] for p in parts]
    mean = ((sums[0] + sums[1]) + (sums[2] + sums[3])) / whole
    square = (squares[0] + squares[1]) + (squares[2] + squares[3])
    for s, n in zip(sums, numbers):
        away = s / n - mean
        square = square + away * away * n
    mi_ref[0:1, :] = mean - sums[0] / numbers[0] if centered else mean
    mi_ref[1:2, :] = lax.rsqrt(square / whole + EPS)


def merged_sums(parts, out_ref):
    out_ref[...] = (parts[0][...] + parts[1][...]) + (parts[2][...] + parts[3][...])


class Weights:
    def __init__(self, section, place_ref, sources, buffer, sems):
        self.buffer, self.sems = buffer, sems
        self.piece = buffer.shape[0] // 4
        self.own = own = sources[0]
        first, second, third, other_first, other_second, other_third = sources[1:]
        relative = place_ref[0] ^ section
        core = place_ref[1]
        straight = relative == 1 + core
        near = (relative == 1) | (relative == 2)

        @pl.when(relative == 0)
        def _():
            for i in range(4):
                pltpu.make_async_copy(own.at[pl.ds(i * self.piece, self.piece)], self.part(i), sems.at[i]).start()

        def fetch(mine, other):
            for i in range(4):
                source, side = (mine, core) if i < 2 else (other, 1 - core)
                at = side * 2 + i % 2
                rows = pl.ds(i % 2 * self.piece, self.piece)
                pltpu.make_async_copy(source.at[rows], self.part(at), sems.at[at]).start()

        @pl.when(near & straight)
        def _():
            fetch(first, other_second)

        @pl.when(near & jnp.logical_not(straight))
        def _():
            fetch(second, other_first)

        @pl.when(relative == 3)
        def _():
            fetch(third, other_third)

    def part(self, at):
        start = at * self.piece
        if not isinstance(at, int):
            start = pl.multiple_of(start, 16)
        return self.buffer.at[pl.ds(start, self.piece)]

    def wait(self, at):
        source = self.own.at[pl.ds(0, self.piece)]
        pltpu.make_async_copy(source, self.part(at), self.sems.at[at]).wait()


def blocks(width, count=4):
    size = width // count
    return [pl.ds(i * size, size) for i in range(count)]


def first_kernel(section, place, k0, u, mask, *rest):
    sources, (z, st, w, sems) = rest[:7], rest[7:]
    weights = Weights(section, place, sources, w, sems)
    for i, cols in enumerate(blocks(u.shape[1])):
        weights.wait(i)
        part = jnp.dot(u[:, cols], w[cols, :], preferred_element_type=f32)
        z[...] = part if i == 0 else z[...] + part
    local_moments(z, pl.ds(0, z.shape[1]), mask, k0[0:1, 0:1], st)


def shifted_copies(values, column):
    left = jnp.where(column >= 1, pltpu.roll(values, 1, 0), 0.0)
    right = jnp.where(column < FRAME - 1, pltpu.roll(values, PIX - 1, 0), 0.0)
    return left, values, right


def clear_borders(buffer):
    images, rows, width = buffer.shape
    zero = jnp.zeros((images, PAD, width), bf16)
    buffer[:, 0:PAD, :] = zero
    buffer[:, rows - PAD : rows, :] = zero


def frame_column(width):
    return lax.broadcasted_iota(jnp.int32, (PIX, width), 0) % FRAME


def middle_kernel(section, place, k0, k1, k2, k3, z1, p0, p1, p2, p3, gain, bias, mask, *rest):
    sources, (hs, z2, st, mi, ka, kt, sems_a, sems_t) = rest[:7], rest[7:]
    lower = Weights(section, place, sources, ka, sems_a)
    upper = Weights(section + 1, place, sources, kt, sems_t)
    merged_moments((p0, p1, p2, p3), (k0, k1, k2, k3), mi)
    clear_borders(hs)
    images = hs.shape[0]
    half = z1.shape[1] // 2
    column = frame_column(128)

    def one(image, carry):
        r = pl.ds(pl.multiple_of(image * PIX, PIX), PIX)
        for j in range(z1.shape[1] // 128):
            cols = pl.ds(j * 128, 128)
            n = (z1[r, cols] - mi[0:1, cols]) * mi[1:2, cols]
            a = n * gain[:, cols] + bias[:, cols]
            h = a * sigmoid(a) * mask[r, :]
            side, inner = divmod(j * 128, half)
            for k, copy in enumerate(shifted_copies(h, column)):
                hs[image, PAD : PAD + PIX, pl.ds(side * 3 * half + k * half + inner, 128)] = copy.astype(bf16)
        return carry

    lax.fori_loop(0, images, one, 0)
    for weights in (lower, upper):
        for i in range(4):
            weights.wait(i)
    rows = z1.shape[0]
    for d in range(3):
        taps = hs[:, FRAME * d : FRAME * d + PIX, :].reshape(rows, 6 * half)
        ks = pl.ds(3 * half * d, 3 * half)
        part = jnp.dot(taps[:, : 3 * half], ka[ks, :], preferred_element_type=f32)
        part = part + jnp.dot(taps[:, 3 * half :], kt[ks, :], preferred_element_type=f32)
        z2[...] = part if d == 0 else z2[...] + part
    local_moments(z2, pl.ds(0, z2.shape[1]), mask, k0[0:1, 0:1], st)


def expand_kernel(section, place, k0, k1, k2, k3, z2, p0, p1, p2, p3, gain, bias, mask, *rest):
    sources, (h2, z3, st, mi, w, z, sems) = rest[:7], rest[7:]
    weights = Weights(section, place, sources, w, sems)
    merged_moments((p0, p1, p2, p3), (k0, k1, k2, k3), mi)

    def one(r, carry):
        n = (z2[r, :] - mi[0:1, :]) * mi[1:2, :]
        a = n * gain[...] + bias[...]
        h2[r, :] = (a * sigmoid(a) * mask[r, :]).astype(bf16)
        return carry

    over_rows(z2.shape[0], one, 0)
    for i, cols in enumerate(blocks(z3.shape[1])):
        weights.wait(i)
        z[...] = lax.dot_general(h2[...], w[cols, :], last_only, preferred_element_type=f32)
        local_moments(z, pl.ds(0, z.shape[1]), mask, k0[0:1, 0:1], st, z3, cols)


def join_kernel(section, place, k0, k1, k2, k3, z3, p0, p1, p2, p3, gain, bias, u, mask, *rest):
    sources, (y, z, st, mi, w, sems) = rest[:7], rest[7:]
    weights = Weights(section, place, sources, w, sems)
    merged_moments((p0, p1, p2, p3), (k0, k1, k2, k3), mi, True)
    for i, cols in enumerate(blocks(z3.shape[1])):

        def one(r, carry, cols=cols):
            n = (z3[r, cols].astype(f32) - mi[0:1, cols]) * mi[1:2, cols]
            s = n * gain[:, cols] + bias[:, cols] + u[r, cols].astype(f32)
            y[r, cols] = (s * sigmoid(s) * mask[r, :]).astype(bf16)
            return carry

        over_rows(z3.shape[0], one, 0)
        weights.wait(i)
        part = jnp.dot(y[:, cols], w[cols, :], preferred_element_type=f32)
        z[...] = part if i == 0 else z[...] + part
    local_moments(z, pl.ds(0, z.shape[1]), mask, k0[0:1, 0:1], st)


def slope_of(s):
    part = sigmoid(s)
    return part, part * (1.0 + s * (1.0 - part))


def turn_kernel(k0, k1, k2, k3, z3, p0, p1, p2, p3, gain, bias, u, mask, merged, head, cot, ds, sums, logits, hgrad, mi, y):
    merged_moments((p0, p1, p2, p3), (k0, k1, k2, k3), mi, True)
    for i, cols in enumerate(blocks(z3.shape[1])):
        width = cols.size

        def one(r, carry, cols=cols):
            n = (z3[r, cols].astype(f32) - mi[0:1, cols]) * mi[1:2, cols]
            s = n * gain[:, cols] + bias[:, cols] + u[r, cols].astype(f32)
            part, slope = slope_of(s)
            y[r, :] = (s * part * mask[r, :]).astype(bf16)
            d = merged[r, cols].astype(f32) * mask[r, :] * slope
            ds[r, cols] = d.astype(bf16)
            return carry[0] + fold(d), carry[1] + fold(d * n)

        zero = jnp.zeros((8, width), f32)
        both = over_rows(z3.shape[0], one, (zero, zero))
        sums[0:1, cols] = column_sum(both[0])
        sums[1:2, cols] = column_sum(both[1])
        part = lax.dot_general(head[:, cols], y[...], last_only, preferred_element_type=f32)
        logits[...] = part if i == 0 else logits[...] + part
        for image in range(cot.shape[0]):
            r = pl.ds(image * PIX, PIX)
            part = jnp.dot(cot[image], y[r, :], preferred_element_type=f32)
            grad = part if image == 0 else grad + part
        for side in range(2):
            size = grad.shape[0] // 2
            hgrad[side, i % 2 * 2 + i // 2] = grad[side * size : (side + 1) * size].astype(bf16)


def shrink_kernel(place, number, ds, z3, q0, q1, q2, q3, mi3, gain3, mask, z2, mi2, gain2, bias2, w, dz3, d2, sums, tot):
    merged_sums((q0, q1, q2, q3), tot)
    for i, cols in enumerate(blocks(ds.shape[1])):
        g = gain3[:, cols] * mi3[1:2, cols]
        c1 = g * tot[0:1, cols] / number[0:1, 0:1]
        c2 = g * tot[1:2, cols] / number[0:1, 0:1]

        def one(r, carry, cols=cols, g=g, c1=c1, c2=c2):
            n = (z3[r, cols].astype(f32) - mi3[0:1, cols]) * mi3[1:2, cols]
            d = g * ds[r, cols].astype(f32) - (c1 + n * c2)
            dz3[r, cols] = (mask[r, :] * d).astype(bf16)
            return carry

        over_rows(ds.shape[0], one, 0)
        part = jnp.dot(dz3[:, cols], w[cols, :], preferred_element_type=f32)
        d2[...] = part if i == 0 else d2[...] + part
    narrow_back(d2, z2, mi2, gain2, bias2, mask, sums)


def narrow_back(d, z, mi, gain, bias, mask, sums):
    zero = jnp.zeros((8, z.shape[1]), f32)

    def one(r, carry):
        n = (z[r, :] - mi[0:1, :]) * mi[1:2, :]
        slope = slope_of(n * gain[...] + bias[...])[1]
        value = d[r, :] * mask[r, :] * slope
        d[r, :] = value
        return carry[0] + fold(value), carry[1] + fold(value * n)

    both = over_rows(z.shape[0], one, (zero, zero))
    sums[0:1, :] = column_sum(both[0])
    sums[1:2, :] = column_sum(both[1])


def unmix_kernel(place, number, d2, q0, q1, q2, q3, z2, mi2, gain2, mask, z1, mi1, gain1, bias1, ka, kt, dz2, d1, sums, tot, gs):
    merged_sums((q0, q1, q2, q3), tot)
    clear_borders(gs)
    images = gs.shape[0]
    rows, width = z2.shape
    half = width // 2
    column = frame_column(128)

    def one(image, carry):
        r = pl.ds(pl.multiple_of(image * PIX, PIX), PIX)
        for j in range(width // 128):
            cols = pl.ds(j * 128, 128)
            g = gain2[:, cols] * mi2[1:2, cols]
            c1 = g * tot[0:1, cols] / number[0:1, 0:1]
            c2 = g * tot[1:2, cols] / number[0:1, 0:1]
            n = (z2[r, cols] - mi2[0:1, cols]) * mi2[1:2, cols]
            d = mask[r, :] * (g * d2[r, cols] - (c1 + n * c2))
            dz2[r, cols] = d.astype(bf16)
            for k, copy in enumerate(shifted_copies(d, column)):
                gs[image, PAD : PAD + PIX, pl.ds(k * width + j * 128, 128)] = copy.astype(bf16)
        return carry

    lax.fori_loop(0, images, one, 0)
    for d in range(3):
        for k in range(3):
            moved = gs[:, FRAME * (2 - d) : FRAME * (2 - d) + PIX, pl.ds((2 - k) * width, width)]
            moved = moved.reshape(rows, width)
            tap = pl.ds((3 * d + k) * half, half)
            for side, kernel in enumerate((ka, kt)):
                cols = pl.ds(side * half, half)
                part = lax.dot_general(moved, kernel[tap, :], last_only, preferred_element_type=f32)
                d1[:, cols] = part if d + k == 0 else d1[:, cols] + part
    narrow_back(d1, z1, mi1, gain1, bias1, mask, sums)


def narrow_finish(d1, q, z1, mi1, gain1, mask, number, dz1, tot):
    merged_sums(q, tot)
    g = gain1[...] * mi1[1:2, :]
    c1 = g * tot[0:1, :] / number[0:1, 0:1]
    c2 = g * tot[1:2, :] / number[0:1, 0:1]

    def one(r, carry):
        n = (z1[r, :] - mi1[0:1, :]) * mi1[1:2, :]
        dz1[r, :] = (mask[r, :] * (g * d1[r, :] - (c1 + n * c2))).astype(bf16)
        return carry

    over_rows(z1.shape[0], one, 0)


def widen_kernel(place, number, d1, q0, q1, q2, q3, z1, mi1, gain1, mask, ds, z3, mi3, gain3, bias3, u, w, dz1, ds0, sums, tot, du):
    narrow_finish(d1, (q0, q1, q2, q3), z1, mi1, gain1, mask, number, dz1, tot)
    for i, cols in enumerate(blocks(ds.shape[1])):
        du[...] = lax.dot_general(dz1[...], w[cols, :], last_only, preferred_element_type=f32)

        def one(r, carry, cols=cols):
            dy = (du[r, :] + ds[r, cols].astype(f32)).astype(bf16).astype(f32)
            n = (z3[r, cols].astype(f32) - mi3[0:1, cols]) * mi3[1:2, cols]
            s = n * gain3[:, cols] + bias3[:, cols] + u[r, cols].astype(f32)
            d = dy * mask[r, :] * slope_of(s)[1]
            ds0[r, cols] = d.astype(bf16)
            return carry[0] + fold(d), carry[1] + fold(d * n)

        zero = jnp.zeros((8, cols.size), f32)
        both = over_rows(ds.shape[0], one, (zero, zero))
        sums[0:1, cols] = column_sum(both[0])
        sums[1:2, cols] = column_sum(both[1])


def last_kernel(place, number, d1, q0, q1, q2, q3, z1, mi1, gain1, mask, ds, w, dz1, keep, give, tot):
    narrow_finish(d1, (q0, q1, q2, q3), z1, mi1, gain1, mask, number, dz1, tot)
    half = keep.shape[0]
    for i, cols in enumerate(blocks(ds.shape[1])):
        block = lax.dot_general(dz1[...], w[cols, :], last_only, preferred_element_type=f32)
        keep[:, cols] = block[:half] + ds[:half, cols].astype(f32)
        give[:, cols] = (block[half:] + ds[half:, cols].astype(f32)).astype(bf16)


def in_place_kernel(where, mine, other, out):
    core, y_side = where[0], where[2]
    size = mine.shape[0] // 2
    for source, side in ((mine, core), (other, 1 - core)):
        for y in range(2):
            at = pl.multiple_of((side * 2 + (y ^ y_side)) * size, 16)
            out[pl.ds(at, size), :] = source[pl.ds(y * size, size), :].astype(f32)


def first_mix_kernel(shares, where, *refs):
    give, keep = refs[-2:]
    core, x_side, y_side = where[0], where[1], where[2]
    for section in range(2):
        for half in range(2):
            kept = jnp.where(core == 0, section == x_side, half == y_side)
            at = jnp.where(core == 0, half, section)
            for out, chosen in ((keep, kept), (give, jnp.logical_not(kept))):

                @pl.when(chosen)
                def _(out=out, at=at, section=section, half=half):
                    start = 0
                    for k, share in enumerate(shares):
                        own, other = refs[4 * k + 2 * section : 4 * k + 2 * section + 2]
                        rows = pl.ds(half * share, share)
                        value = own[rows, :].astype(f32) + other[rows, :].astype(f32)
                        out[at, pl.ds(start, share), :] = value.astype(bf16)
                        start += share


def second_mix_kernel(where, keep, got, give_out, keep_out):
    for at in range(2):
        for out, chosen in ((keep_out, at == where[0]), (give_out, at != where[0])):

            @pl.when(chosen)
            def _(out=out):
                out[...] = (keep[at].astype(f32) + got[at].astype(f32)).astype(bf16)


def drop_kernel(codes, cots, head, merged):
    line = lax.broadcasted_iota(jnp.int32, cots.shape[1:], 0)
    bounds = (0, KSEG, KSEG + KDEP, KSEG + KDEP + KNOR)
    cot = cots[0].astype(f32)
    tasks = [
        jnp.where((line >= a) & (line < b), cot, 0.0).T.astype(bf16)
        for a, b in zip(bounds[:-1], bounds[1:])
    ]
    for cols in blocks(head.shape[1], 8):
        g = [jnp.dot(task, head[:, cols], preferred_element_type=f32) for task in tasks]
        total = g[0] + g[1] + g[2]
        magnitude = sum(jnp.sqrt(v * v + DROP_FLOOR * DROP_FLOOR) for v in g)
        purity = 0.5 + 0.5 * (total / magnitude)
        bar = (codes[0, :, cols] + 0.5) / CODE_SCALE
        keep = sigmoid((purity - bar) * DROP_SHARPNESS)
        lose = 1.0 - keep
        value = sum(v * jnp.where(v > 0.0, keep, lose) for v in g)
        merged[:, cols] = value.astype(bf16)


VM = pl.BlockSpec(memory_space=pltpu.VMEM)
SM = pl.BlockSpec(memory_space=pltpu.SMEM)
ANY = pl.BlockSpec(memory_space=pltpu.HBM)


def run(kernel, operands, specs, outs, scratch, flops):
    return pl.pallas_call(
        kernel,
        out_shape=[jax.ShapeDtypeStruct(shape, kind) for shape, kind in outs],
        in_specs=specs,
        out_specs=[VM] * len(outs),
        scratch_shapes=scratch,
        compiler_params=pltpu.CompilerParams(vmem_limit_bytes=LIMIT),
        cost_estimate=pl.CostEstimate(
            flops=SCALE * flops,
            bytes_accessed=SCALE * sum(o.size * o.dtype.itemsize for o in operands[:16]),
            transcendentals=0,
        ),
    )(*operands)


def flip(value, bits):
    count = lax.axis_size("dp")
    return lax.ppermute(value, "dp", [(i, i ^ bits) for i in range(count)])


def cross(value, bits):
    count = lax.axis_size("segment")
    return lax.ppermute(value, "segment", [(i, i ^ bits) for i in range(count)])


def turned(value, even, odd):
    size, count = lax.axis_size("segment"), lax.axis_size("dp")
    pairs = [
        (i * count + j, (i ^ (odd if j % 2 else even)) * count + j) for i in range(size) for j in range(count)
    ]
    return lax.ppermute(value, ("segment", "dp"), pairs)


def after(value, *others):
    return lax.optimization_barrier((value,) + others)[0]


def dp_bits():
    count = lax.axis_size("dp")
    return [1 << k for k in range(count.bit_length() - 1)]


def group_bits():
    bits = [b for b in dp_bits() if b != SWAP]
    return bits[:2], bits[2:]


def four_parts(value):
    first, _ = group_bits()
    near = jnp.stack([value, flip(value, first[0])])
    far = flip(near, first[1])
    return [near[0], near[1], far[0], far[1]]


def pair_up(stats, count):
    for b in group_bits()[1]:
        other, other_count = flip(stats, b), flip(count, b)
        whole = count + other_count
        here, there = count[0, 0], other_count[0, 0]
        away = stats[0] / here - other[0] / there
        square = stats[1] + other[1] + away * away * (here * there / (here + there))
        merged = jnp.stack([stats[0] + other[0], square])
        if stats.shape[0] > 2:
            merged = jnp.concatenate([merged, stats[2:] + other[2:]], axis=0)
        stats, count = merged, whole
    return stats


def pair_sum(value):
    for b in group_bits()[1]:
        value = value + flip(value, b)
    return value


def split_rows(value, index, parts=2):
    size = value.shape[0] // parts
    return lax.dynamic_slice_in_dim(value, index * size, size, 0)


def on_device(
    inputs,
    extents,
    wide_weight,
    mid_weight,
    narrow_gain,
    narrow_bias,
    expand_gain,
    expand_bias,
    head_weight,
    head_cotangent,
    drop_codes,
):
    seg = lax.axis_index("segment")
    dp = lax.axis_index("dp")
    sections = lax.axis_size("segment")
    x_side, y_side, core = seg % 2, seg // 2, dp % 2
    swapped = (dp // SWAP) % 2
    channels = inputs.shape[-1]
    narrow = wide_weight.shape[-1]
    half_width = narrow // 2
    classes = head_weight.shape[-1]
    place = jnp.stack([seg, core]).astype(jnp.int32)

    own_small = jnp.concatenate(
        [head_weight.T, jnp.zeros((HEADS - classes, head_weight.shape[0]), bf16), expand_gain.T, expand_bias.T]
        + [narrow_gain, narrow_bias, jnp.zeros((10, narrow), bf16)],
        axis=0,
    )
    small_x = cross(own_small, 1)
    small_y = cross(jnp.stack([own_small, small_x]), 2)
    small = jnp.stack([own_small, small_x, small_y[0], small_y[1]])
    small = jnp.stack([lax.dynamic_index_in_dim(small, k ^ seg, 0, keepdims=False) for k in range(4)])
    lanes = jnp.moveaxis(small[:, : HEADS + 4], 0, 1).reshape(HEADS + 4, channels)
    head_rows = lanes[:HEADS]
    gain_wide = lanes[HEADS : HEADS + 2].astype(f32)
    bias_wide = lanes[HEADS + 2 : HEADS + 4].astype(f32)
    gain_narrow = small[:, HEADS + 4].astype(f32)
    bias_narrow = small[:, HEADS + 5].astype(f32)

    own_count = inputs.shape[0]
    start = seg * own_count

    def own_part(value):
        return lax.dynamic_slice_in_dim(value, start, own_count, 0).astype(f32).reshape(own_count, -1, PIX)

    boxes = jnp.pad(extents, ((0, 0), (0, 0), (0, PIX - 2)))
    facts = jnp.concatenate([own_part(v) for v in (head_cotangent, drop_codes, boxes)], axis=1)
    facts = jnp.pad(facts, ((0, 0), (0, -facts.shape[1] % 8), (0, 0)))
    keep_facts = lax.dynamic_index_in_dim(facts, swapped, 0, keepdims=False)
    got_facts = flip(lax.dynamic_index_in_dim(facts, 1 - swapped, 0, keepdims=False), SWAP)
    facts = jnp.stack([keep_facts, got_facts])
    code_rows = channels // PIX
    cotangent = facts[:, :classes].astype(bf16)
    codes = facts[:, classes : classes + code_rows].reshape(2, 1, channels)
    box = facts[:, classes + code_rows, :2].astype(jnp.int32)
    keep_in = lax.dynamic_index_in_dim(inputs, swapped, 0, keepdims=False)
    give_in = lax.dynamic_index_in_dim(inputs, 1 - swapped, 0, keepdims=False)
    half_pix = PIX // 2
    got_in = [flip(give_in[:, :half_pix], SWAP)]
    images = 2 * inputs.shape[1]
    rows = images * PIX

    wide_own = wide_weight[0]
    mid_own = mid_weight[0].reshape(-1, narrow)

    def exchange(own, *gate):
        mine = after(split_rows(own, core), *gate)
        return turned(mine, 1, 2), turned(mine, 2, 1)

    def pass_on(own, first, second, gate, flip_gate=()):
        pieces = [first, second, turned(after(first, second, *gate), 2, 1)]
        return [own] + pieces + [flip(after(p, *flip_gate), 1) for p in pieces]

    wide = pass_on(wide_own, *exchange(wide_own, give_in), (got_in[0], small_x, got_facts))
    got_in.append(flip(after(give_in[:, half_pix:], got_in[0], wide[4], wide[5]), SWAP))
    mid_two = exchange(mid_own, wide[1], wide[2])

    local_count = jnp.full((8, 128), jnp.sum(box[:, 0] * box[:, 1]).astype(f32))
    position = jnp.arange(PIX, dtype=jnp.int32)
    inside = (position // FRAME < box[:, 0:1]) & (position % FRAME < box[:, 1:2])
    mask = inside.astype(f32).reshape(rows, 1)

    cot_columns = jnp.pad(cotangent, ((0, 0), (0, HEADS - classes), (0, 0)))
    (merged,) = pl.pallas_call(
        drop_kernel,
        grid=(images,),
        in_specs=[
            pl.BlockSpec((1, 1, channels), lambda i: (i, 0, 0)),
            pl.BlockSpec((1, HEADS, PIX), lambda i: (i, 0, 0)),
            pl.BlockSpec((HEADS, channels), lambda i: (0, 0)),
        ],
        out_specs=[pl.BlockSpec((PIX, channels), lambda i: (i, 0))],
        out_shape=[jax.ShapeDtypeStruct((rows, channels), bf16)],
        compiler_params=pltpu.CompilerParams(vmem_limit_bytes=LIMIT),
    )(codes, cot_columns, head_rows)

    got_in = jnp.concatenate([got_in[0], after(got_in[1], merged)], axis=1)
    entry = jnp.concatenate([keep_in, got_in], axis=0).reshape(rows, channels)

    narrow_f = ((rows, narrow), f32)
    narrow_b = ((rows, narrow), bf16)
    wide_f = ((rows, channels), f32)
    wide_b = ((rows, channels), bf16)
    pair_n = ((2, narrow), f32)
    pair_w = ((2, channels), f32)
    copies_b = ((images, PIX + 2 * PAD, 3 * narrow), bf16)
    w_out = ((channels, narrow), bf16)
    m_out = ((9 * half_width, narrow), bf16)
    w_scratch = [None, pltpu.SemaphoreType.DMA((4,))]
    m_scratch = [pltpu.SemaphoreType.DMA((4,)), pltpu.SemaphoreType.DMA((4,))]
    w_specs = [ANY] * 7
    product = 2 * rows * channels * narrow
    conv = 2 * rows * 9 * narrow * narrow

    def row(values, k):
        return values[k : k + 1]

    met = {}

    def moments(stats):
        if id(stats) not in met:
            met[id(stats)] = (four_parts(pair_up(stats, local_count)), stats)
        return met[id(stats)][0]

    kept = {}
    z1, st, w_head = run(
        functools.partial(first_kernel, 0),
        [place, local_count, entry, mask] + wide,
        [SM, VM, VM, VM] + w_specs,
        [narrow_f, ((8, narrow), f32), w_out],
        w_scratch[1:],
        product,
    )
    group_counts = moments(st)
    mid = pass_on(mid_own, *mid_two, (merged, z1), group_counts)
    number = sum(g[2:3, :128] for g in group_counts)
    group_counts = [g[2:3, :128] for g in group_counts]
    u = entry
    for k in range(2):
        head, tail = 2 * k, 2 * k + 1
        hs, z2, st2, mi1, ka, kt = run(
            functools.partial(middle_kernel, head),
            [place] + group_counts + [z1] + moments(st) + [row(gain_narrow, head), row(bias_narrow, head), mask] + mid,
            [SM] + [VM] * 12 + w_specs,
            [copies_b, narrow_f, pair_n, pair_n, m_out, m_out],
            m_scratch,
            conv,
        )
        h2, z3, st3, mi2, w_tail = run(
            functools.partial(expand_kernel, tail),
            [place] + group_counts + [z2] + moments(st2) + [row(gain_narrow, tail), row(bias_narrow, tail), mask] + wide,
            [SM] + [VM] * 12 + w_specs,
            [narrow_b, wide_b, pair_w, pair_n, w_out],
            [pltpu.VMEM((rows, channels // 4), f32), w_scratch[1]],
            product,
        )
        kept[k] = dict(z1=z1, mi1=mi1, hs=hs, z2=z2, mi2=mi2, h2=h2, z3=z3, u=u, ka=ka, kt=kt, w_head=w_head, w_tail=w_tail)
        last = [row(gain_wide, k), row(bias_wide, k), u, mask]
        if k == 0:
            u, z1, st, kept[0]["mi3"], w_head = run(
                functools.partial(join_kernel, 2),
                [place] + group_counts + [z3] + moments(st3) + last + wide,
                [SM] + [VM] * 13 + w_specs,
                [wide_b, narrow_f, pair_n, pair_w, w_out],
                w_scratch[1:],
                product,
            )
        else:
            ds, sums3, logits, head_grad, mi3 = run(
                turn_kernel,
                group_counts + [z3] + moments(st3) + last + [merged, head_rows, cot_columns],
                [VM] * 16,
                [wide_b, pair_w, ((HEADS, rows), f32), ((2, 4, HEADS // 2, channels // 4), bf16), pair_w],
                [pltpu.VMEM((rows, channels // 4), bf16)],
                product // 4,
            )
            kept[1]["mi3"] = mi3

    grads, totals = {}, {}

    def plus(a, b):
        return (a.astype(f32) + b.astype(f32)).astype(bf16)

    def joined(side, mine, other):
        return jnp.where(
            side == 1, jnp.concatenate([other, mine], axis=0), jnp.concatenate([mine, other], axis=0)
        )

    second_side = jnp.where(core == 0, y_side, x_side).astype(jnp.int32)
    sides = jnp.stack([core, x_side, y_side]).astype(jnp.int32)

    class Chain:
        def __init__(self, kinds):
            shares = tuple(kind[0].shape[0] // 2 for kind in kinds)
            shape = jax.ShapeDtypeStruct((2, sum(shares), narrow), bf16)
            operands = [value for kind in kinds for value in kind]
            self.give, self.keep = pl.pallas_call(
                functools.partial(first_mix_kernel, shares),
                in_specs=[SM] + [VM] * len(operands),
                out_specs=[VM, VM],
                out_shape=[shape, shape],
                compiler_params=pltpu.CompilerParams(vmem_limit_bytes=LIMIT),
            )(sides, *operands)
            self.todo = ["first", "second"]
            self.todo += ["in", "mid", "out"] if z_chips == 4 else [("meet", b) for b in dp_bits()[1:]]

        def send(self):
            step = self.todo.pop(0)
            if step == "first":
                self.got = turned(self.give, 1, 2)
            elif step == "second":
                self.got = turned(self.give, 2, 1)
            elif isinstance(step, tuple):
                self.got = flip(self.part, step[1])
            else:
                ways = {"in": [(0, 1), (3, 2)], "mid": [(1, 2), (2, 1)], "out": [(1, 0), (2, 3)]}[step]
                self.got = line_send(self.part, ways)
            self.step = step
            return self.got

        def take(self, *holds):
            got = after(self.got, *holds)
            if self.todo[:1] == ["second"]:
                shape = jax.ShapeDtypeStruct(got.shape[1:], bf16)
                self.give, self.keep = pl.pallas_call(
                    second_mix_kernel,
                    in_specs=[SM, VM, VM],
                    out_specs=[VM, VM],
                    out_shape=[shape, shape],
                    compiler_params=pltpu.CompilerParams(vmem_limit_bytes=LIMIT),
                )(second_side.reshape(1), self.keep, got)
                return self.give
            if self.step == "second":
                self.part = plus(self.keep, got)
            elif self.step == "out":
                self.part = jnp.where((z_place == 1) | (z_place == 2), self.part, got)
            else:
                self.part = plus(self.part, got)
            return self.part

    z_chips = lax.axis_size("dp") // 2
    z_place = dp // 2

    def line_send(value, ways):
        return lax.ppermute(value, "dp", [(2 * a + c, 2 * b + c) for a, b in ways for c in range(2)])

    def to_owner(part, part1):
        keep = jnp.where(y_side == 0, part, part1)
        return jnp.concatenate([keep, cross(jnp.where(y_side == 0, part1, part), 2)])

    def in_place(half):
        (out,) = pl.pallas_call(
            in_place_kernel,
            in_specs=[SM, VM, VM],
            out_specs=[VM],
            out_shape=[jax.ShapeDtypeStruct((2 * half.shape[0], narrow), f32)],
            compiler_params=pltpu.CompilerParams(vmem_limit_bytes=LIMIT),
        )(sides, half, flip(half, 1))
        return out

    def tile_grad(left, right, dims=rows_only):
        return lax.dot_general(left, right, dims, preferred_element_type=f32).astype(bf16)

    def conv_grad(hs, dz2, side):
        right = dz2.reshape(images, PIX, narrow)
        both = (((0, 1), (0, 1)), ((), ()))
        width = 3 * half_width
        parts = [
            tile_grad(hs[:, FRAME * d : FRAME * d + PIX, side * width : (side + 1) * width], right, both)
            for d in range(3)
        ]
        whole = jnp.concatenate(parts, axis=0)
        return split_rows(whole, core), flip(split_rows(whole, 1 - core), 1)

    def sections_of(kind, k):
        return [v for i in range(2) for v in grads[kind, 2 * k + i]]

    def split_grad(left, right):
        size = left.shape[1] // 2
        mine, other = [tile_grad(lax.dynamic_slice_in_dim(left, c * size, size, 1), right) for c in (core, 1 - core)]
        return mine, flip(other, 1)

    for k in (1, 0):
        head, tail = 2 * k, 2 * k + 1
        it = kept[k]
        narrow2 = [it["z2"], it["mi2"], row(gain_narrow, tail)]
        narrow1 = [it["z1"], it["mi1"], row(gain_narrow, head)]
        dz3, d2, sums2, totals["wide", k] = run(
            shrink_kernel,
            [place if k else first_hold, number, ds, it["z3"]] + four_parts(pair_sum(sums3)) + [it["mi3"], row(gain_wide, k), mask]
            + narrow2 + [row(bias_narrow, tail), it["w_tail"]],
            [SM] + [VM] * 15,
            [wide_b, narrow_f, pair_n, pair_w],
            [],
            product,
        )
        grads["w", tail] = split_grad(dz3, it["h2"])
        parts2 = four_parts(pair_sum(sums2))
        hold = place
        if k == 0:
            hold = after(place, m1.take(), w1.take(m1.part))
            w1.send()
        dz2, d1, sums1, totals["narrow", tail] = run(
            unmix_kernel,
            [hold, number, d2] + parts2 + narrow2 + [mask] + narrow1
            + [row(bias_narrow, head), it["ka"], it["kt"]],
            [SM] + [VM] * 16,
            [narrow_b, narrow_f, pair_n, pair_n],
            [pltpu.VMEM(*copies_b)],
            conv,
        )
        parts1 = four_parts(pair_sum(sums1))
        grads["m", head] = conv_grad(it["hs"], dz2, 0)
        grads["m", tail] = conv_grad(it["hs"], dz2, 1)
        hold = place
        if k == 1:
            m1 = Chain([sections_of("m", 1)])
            m1.send()
            hold = after(place, m1.give)
        else:
            m0 = Chain([sections_of("m", 0)])
            hold = after(place, w1.take(), m0.give)
            m1.part = after(m1.part, *parts1)
            m1.send()
            m0.send()
        base = [hold, number, d1] + parts1 + narrow1 + [mask, ds]
        if k == 1:
            low = kept[0]
            dz1, ds, sums3, totals["narrow", head] = run(
                widen_kernel,
                base + [low["z3"], low["mi3"], row(gain_wide, 0), row(bias_wide, 0), low["u"], it["w_head"]],
                [SM] + [VM] * 17,
                [narrow_b, wide_b, pair_w, pair_n],
                [pltpu.VMEM((rows, channels // 4), f32)],
                product,
            )
            grads["w", head] = split_grad(it["u"], dz1)
        else:
            dz1, grad_keep, grad_give, totals["narrow", head] = run(
                last_kernel,
                base + [it["w_head"]],
                [SM] + [VM] * 12,
                [narrow_b, ((rows // 2, channels), f32), ((rows // 2, channels), bf16), pair_n],
                [],
                product,
            )
            grads["w", head] = split_grad(it["u"], dz1)
        if k == 1:
            own = lax.dynamic_index_in_dim(head_grad, core, 0, keepdims=False)
            other = flip(lax.dynamic_index_in_dim(head_grad, 1 - core, 0, keepdims=False), 1)
            extra = [v[2 * i : 2 * i + 2].reshape(-1, narrow) for i in range(2) for v in (own, other)]
            w1 = Chain([sections_of("w", 1), extra])
            w1.send()
            first_hold = after(place, m1.take(), w1.give)
            m1.send()
    flat = jnp.concatenate(
        [totals["wide", k].reshape(-1, narrow) for k in range(2)]
        + [totals["narrow", i] for i in range(sections)],
        axis=0,
    )
    def returned(keep, got):
        got = got.astype(f32)
        return jnp.stack([jnp.where(swapped == 0, keep, got), jnp.where(swapped == 0, got, keep)])

    by_pair = z_chips == 4 and SWAP == 2
    home = line_send(grad_give, [(1, 0), (2, 3)]) if by_pair else flip(grad_give, SWAP)
    w0 = Chain([sections_of("w", 0)])
    w0.send()
    tick = m0.take(w0.give)
    m0.send()
    tick = m1.take(tick)
    m1.send()
    w1.part = after(w1.part, tick)
    w1.send()
    tick = m0.take(tick)
    m0.send()
    tick = w0.take(tick)
    w0.send()
    tick = m1.take(tick, home)
    m1.send()
    tick = w1.take(tick)
    w1.send()
    tick = w0.take(tick)
    w0.send()
    tick = m0.take(tick)
    m0.send()
    if by_pair:
        back = line_send(after(grad_give, tick), [(0, 1), (3, 2)])
        home = jnp.where((z_place == 0) | (z_place == 3), home, back)
    flat = after(flat, tick)
    flat = flat + cross(flat, 1)
    tick = m1.take(tick)
    tick = w1.take(tick)
    w1.send()
    tick = w0.take(tick, flat)
    w0.send()
    flat = flat + cross(flat, 2)
    tick = m0.take(tick)
    m0.send()
    tick = w1.take(tick)
    edge = wide_own.shape[0] // 4
    heads = joined(core, w1.part[edge:], flip(w1.part[edge:], 1))
    tick = w0.take(tick, flat)
    w0.send()
    by_image = after(logits, tick)[:classes].reshape(classes, images, PIX).transpose(1, 0, 2)
    logits_out = returned(by_image[: images // 2], flip(by_image[images // 2 :].astype(bf16), SWAP))
    flat = flat + flip(after(flat, tick), SWAP)
    tick = m0.take(tick, heads)
    mid_half = to_owner(m0.part, m1.part)
    shape = (images // 2, PIX, channels)
    input_grad = returned(grad_keep.reshape(shape), after(home, tick).reshape(shape))
    wide_half = to_owner(w0.take(tick), w1.part[:edge])
    mid_grad = in_place(mid_half)
    wide_grad = in_place(wide_half)

    wide_count = 4 * channels // narrow
    wide_all = flat[:wide_count].reshape(2, 2, channels)
    narrow_all = lax.dynamic_index_in_dim(
        flat[wide_count:].reshape(sections, 2, narrow), seg, 0, keepdims=False
    )
    share = channels // sections
    wide_mine = lax.dynamic_slice_in_dim(wide_all, seg * share, share, 2)

    head_out = heads[:classes].astype(f32).T

    return (
        logits_out,
        input_grad,
        wide_grad[None],
        mid_grad.reshape(1, 9, half_width, narrow),
        narrow_all[1:2],
        narrow_all[0:1],
        wide_mine[:, 1].T,
        wide_mine[:, 0].T,
        head_out,
    )


def solution(mesh):
    return jax.shard_map(
        on_device,
        mesh=mesh,
        in_specs=(
            P("segment", "dp", None, None),
            P(None, "dp", None),
            P("segment", None, None),
            P("segment", None, None, None),
            P("segment", None),
            P("segment", None),
            P("segment", None),
            P("segment", None),
            P("segment", None),
            P(None, "dp", None, None),
            P(None, "dp", None),
        ),
        out_specs=(
            P("segment", "dp", None, None),
            P("segment", "dp", None, None),
            P("segment", None, None),
            P("segment", None, None, None),
            P("segment", None),
            P("segment", None),
            P("segment", None),
            P("segment", None),
            P("segment", None),
        ),
        check_vma=False,
    )
```

```python
import functools

import jax
import jax.numpy as jnp
from jax import lax
from jax.experimental import pallas as pl
from jax.experimental.pallas import tpu as pltpu
from jax.sharding import PartitionSpec as P

KSEG = 40
KDEP = 1
KNOR = 3
FRAME = 16
PIX = FRAME * FRAME
EPS = 1e-05
DROP_FLOOR = 0.01
DROP_SHARPNESS = 8.0
CODE_SCALE = 65536.0
SWAP = 2
STEP = 256
PAD = FRAME
HEADS = 64
LIMIT = 18 << 20
SCALE = 8

f32 = jnp.float32
bf16 = jnp.bfloat16
rows_only = (((0,), (0,)), ((), ()))
last_only = (((1,), (1,)), ((), ()))


def sigmoid(values):
    return 0.5 * jnp.tanh(0.5 * values) + 0.5


def fold(values):
    return jnp.sum(values.reshape(values.shape[0] // 8, 8, values.shape[1]), axis=0)


def over_rows(rows, body, init):
    def one(index, carry):
        return body(pl.ds(pl.multiple_of(index * STEP, STEP), STEP), carry)

    return lax.fori_loop(0, rows // STEP, one, init)


def column_sum(total):
    return jnp.sum(total, axis=0, keepdims=True)


def local_moments(z_ref, cols, mask_ref, count, st_ref, out_ref=None, out_cols=None):
    rows, width = z_ref.shape[0], cols.size
    out_cols = cols if out_cols is None else out_cols
    zero = jnp.zeros((8, width), f32)

    def add(r, total):
        return total + fold(z_ref[r, cols] * mask_ref[r, :])

    total = column_sum(over_rows(rows, add, zero))
    mean = total / count

    def add_square(r, square):
        away = z_ref[r, cols] - mean
        if out_ref is not None:
            out_ref[r, out_cols] = away.astype(bf16)
        return square + fold(away * away * mask_ref[r, :])

    square = column_sum(over_rows(rows, add_square, zero))
    st_ref[0:1, out_cols] = total
    st_ref[1:2, out_cols] = square
    if st_ref.shape[0] > 2:
        st_ref[2:3, out_cols] = jnp.zeros_like(total) + count


def pixels(counts):
    numbers = [c[0:1, 0:1] for c in counts]
    return numbers, (numbers[0] + numbers[1]) + (numbers[2] + numbers[3])


def merged_moments(parts, counts, mi_ref, centered=False):
    numbers, whole = pixels(counts)
    sums = [p[0:1, :] for p in parts]
    squares = [p[1:2, :] for p in parts]
    mean = ((sums[0] + sums[1]) + (sums[2] + sums[3])) / whole
    square = (squares[0] + squares[1]) + (squares[2] + squares[3])
    for s, n in zip(sums, numbers):
        away = s / n - mean
        square = square + away * away * n
    mi_ref[0:1, :] = mean - sums[0] / numbers[0] if centered else mean
    mi_ref[1:2, :] = lax.rsqrt(square / whole + EPS)


def merged_sums(parts, out_ref):
    out_ref[...] = (parts[0][...] + parts[1][...]) + (parts[2][...] + parts[3][...])


class Weights:
    def __init__(self, section, place_ref, sources, buffer, sems):
        self.buffer, self.sems = buffer, sems
        self.piece = buffer.shape[0] // 4
        self.own = own = sources[0]
        first, second, third, other_first, other_second, other_third = sources[1:]
        relative = place_ref[0] ^ section
        core = place_ref[1]
        straight = relative == 1 + core
        near = (relative == 1) | (relative == 2)

        @pl.when(relative == 0)
        def _():
            for i in range(4):
                pltpu.make_async_copy(own.at[pl.ds(i * self.piece, self.piece)], self.part(i), sems.at[i]).start()

        def fetch(mine, other):
            for i in range(4):
                source, side = (mine, core) if i < 2 else (other, 1 - core)
                at = side * 2 + i % 2
                rows = pl.ds(i % 2 * self.piece, self.piece)
                pltpu.make_async_copy(source.at[rows], self.part(at), sems.at[at]).start()

        @pl.when(near & straight)
        def _():
            fetch(first, other_second)

        @pl.when(near & jnp.logical_not(straight))
        def _():
            fetch(second, other_first)

        @pl.when(relative == 3)
        def _():
            fetch(third, other_third)

    def part(self, at):
        start = at * self.piece
        if not isinstance(at, int):
            start = pl.multiple_of(start, 16)
        return self.buffer.at[pl.ds(start, self.piece)]

    def wait(self, at):
        source = self.own.at[pl.ds(0, self.piece)]
        pltpu.make_async_copy(source, self.part(at), self.sems.at[at]).wait()


def blocks(width, count=4):
    size = width // count
    return [pl.ds(i * size, size) for i in range(count)]


def first_kernel(section, place, k0, u, mask, *rest):
    sources, (z, st, w, sems) = rest[:7], rest[7:]
    weights = Weights(section, place, sources, w, sems)
    for i, cols in enumerate(blocks(u.shape[1])):
        weights.wait(i)
        part = jnp.dot(u[:, cols], w[cols, :], preferred_element_type=f32)
        z[...] = part if i == 0 else z[...] + part
    local_moments(z, pl.ds(0, z.shape[1]), mask, k0[0:1, 0:1], st)


def shifted_copies(values, column):
    left = jnp.where(column >= 1, pltpu.roll(values, 1, 0), 0.0)
    right = jnp.where(column < FRAME - 1, pltpu.roll(values, PIX - 1, 0), 0.0)
    return left, values, right


def clear_borders(buffer):
    images, rows, width = buffer.shape
    zero = jnp.zeros((images, PAD, width), bf16)
    buffer[:, 0:PAD, :] = zero
    buffer[:, rows - PAD : rows, :] = zero


def frame_column(width):
    return lax.broadcasted_iota(jnp.int32, (PIX, width), 0) % FRAME


def middle_kernel(section, place, k0, k1, k2, k3, z1, p0, p1, p2, p3, gain, bias, mask, *rest):
    sources, (hs, z2, st, mi, ka, kt, sems_a, sems_t) = rest[:7], rest[7:]
    lower = Weights(section, place, sources, ka, sems_a)
    upper = Weights(section + 1, place, sources, kt, sems_t)
    merged_moments((p0, p1, p2, p3), (k0, k1, k2, k3), mi)
    clear_borders(hs)
    images = hs.shape[0]
    half = z1.shape[1] // 2
    column = frame_column(128)

    def one(image, carry):
        r = pl.ds(pl.multiple_of(image * PIX, PIX), PIX)
        for j in range(z1.shape[1] // 128):
            cols = pl.ds(j * 128, 128)
            n = (z1[r, cols] - mi[0:1, cols]) * mi[1:2, cols]
            a = n * gain[:, cols] + bias[:, cols]
            h = a * sigmoid(a) * mask[r, :]
            side, inner = divmod(j * 128, half)
            for k, copy in enumerate(shifted_copies(h, column)):
                hs[image, PAD : PAD + PIX, pl.ds(side * 3 * half + k * half + inner, 128)] = copy.astype(bf16)
        return carry

    lax.fori_loop(0, images, one, 0)
    for weights in (lower, upper):
        for i in range(4):
            weights.wait(i)
    rows = z1.shape[0]
    for d in range(3):
        taps = hs[:, FRAME * d : FRAME * d + PIX, :].reshape(rows, 6 * half)
        ks = pl.ds(3 * half * d, 3 * half)
        part = jnp.dot(taps[:, : 3 * half], ka[ks, :], preferred_element_type=f32)
        part = part + jnp.dot(taps[:, 3 * half :], kt[ks, :], preferred_element_type=f32)
        z2[...] = part if d == 0 else z2[...] + part
    local_moments(z2, pl.ds(0, z2.shape[1]), mask, k0[0:1, 0:1], st)


def expand_kernel(section, place, k0, k1, k2, k3, z2, p0, p1, p2, p3, gain, bias, mask, *rest):
    sources, (h2, z3, st, mi, w, z, sems) = rest[:7], rest[7:]
    weights = Weights(section, place, sources, w, sems)
    merged_moments((p0, p1, p2, p3), (k0, k1, k2, k3), mi)

    def one(r, carry):
        n = (z2[r, :] - mi[0:1, :]) * mi[1:2, :]
        a = n * gain[...] + bias[...]
        h2[r, :] = (a * sigmoid(a) * mask[r, :]).astype(bf16)
        return carry

    over_rows(z2.shape[0], one, 0)
    for i, cols in enumerate(blocks(z3.shape[1])):
        weights.wait(i)
        z[...] = lax.dot_general(h2[...], w[cols, :], last_only, preferred_element_type=f32)
        local_moments(z, pl.ds(0, z.shape[1]), mask, k0[0:1, 0:1], st, z3, cols)


def join_kernel(section, place, k0, k1, k2, k3, z3, p0, p1, p2, p3, gain, bias, u, mask, *rest):
    sources, (y, z, st, mi, w, sems) = rest[:7], rest[7:]
    weights = Weights(section, place, sources, w, sems)
    merged_moments((p0, p1, p2, p3), (k0, k1, k2, k3), mi, True)
    for i, cols in enumerate(blocks(z3.shape[1])):

        def one(r, carry, cols=cols):
            n = (z3[r, cols].astype(f32) - mi[0:1, cols]) * mi[1:2, cols]
            s = n * gain[:, cols] + bias[:, cols] + u[r, cols].astype(f32)
            y[r, cols] = (s * sigmoid(s) * mask[r, :]).astype(bf16)
            return carry

        over_rows(z3.shape[0], one, 0)
        weights.wait(i)
        part = jnp.dot(y[:, cols], w[cols, :], preferred_element_type=f32)
        z[...] = part if i == 0 else z[...] + part
    local_moments(z, pl.ds(0, z.shape[1]), mask, k0[0:1, 0:1], st)


def slope_of(s):
    part = sigmoid(s)
    return part, part * (1.0 + s * (1.0 - part))


def turn_kernel(k0, k1, k2, k3, z3, p0, p1, p2, p3, gain, bias, u, mask, merged, head, cot, ds, sums, logits, hgrad, mi, y):
    merged_moments((p0, p1, p2, p3), (k0, k1, k2, k3), mi, True)
    for i, cols in enumerate(blocks(z3.shape[1])):
        width = cols.size

        def one(r, carry, cols=cols):
            n = (z3[r, cols].astype(f32) - mi[0:1, cols]) * mi[1:2, cols]
            s = n * gain[:, cols] + bias[:, cols] + u[r, cols].astype(f32)
            part, slope = slope_of(s)
            y[r, :] = (s * part * mask[r, :]).astype(bf16)
            d = merged[r, cols].astype(f32) * mask[r, :] * slope
            ds[r, cols] = d.astype(bf16)
            return carry[0] + fold(d), carry[1] + fold(d * n)

        zero = jnp.zeros((8, width), f32)
        both = over_rows(z3.shape[0], one, (zero, zero))
        sums[0:1, cols] = column_sum(both[0])
        sums[1:2, cols] = column_sum(both[1])
        part = lax.dot_general(head[:, cols], y[...], last_only, preferred_element_type=f32)
        logits[...] = part if i == 0 else logits[...] + part
        for image in range(cot.shape[0]):
            r = pl.ds(image * PIX, PIX)
            part = jnp.dot(cot[image], y[r, :], preferred_element_type=f32)
            grad = part if image == 0 else grad + part
        for side in range(2):
            size = grad.shape[0] // 2
            hgrad[side, i % 2 * 2 + i // 2] = grad[side * size : (side + 1) * size].astype(bf16)


def shrink_kernel(place, number, ds, z3, q0, q1, q2, q3, mi3, gain3, mask, z2, mi2, gain2, bias2, w, dz3, d2, sums, tot):
    merged_sums((q0, q1, q2, q3), tot)
    for i, cols in enumerate(blocks(ds.shape[1])):
        g = gain3[:, cols] * mi3[1:2, cols]
        c1 = g * tot[0:1, cols] / number[0:1, 0:1]
        c2 = g * tot[1:2, cols] / number[0:1, 0:1]

        def one(r, carry, cols=cols, g=g, c1=c1, c2=c2):
            n = (z3[r, cols].astype(f32) - mi3[0:1, cols]) * mi3[1:2, cols]
            d = g * ds[r, cols].astype(f32) - (c1 + n * c2)
            dz3[r, cols] = (mask[r, :] * d).astype(bf16)
            return carry

        over_rows(ds.shape[0], one, 0)
        part = jnp.dot(dz3[:, cols], w[cols, :], preferred_element_type=f32)
        d2[...] = part if i == 0 else d2[...] + part
    narrow_back(d2, z2, mi2, gain2, bias2, mask, sums)


def narrow_back(d, z, mi, gain, bias, mask, sums):
    zero = jnp.zeros((8, z.shape[1]), f32)

    def one(r, carry):
        n = (z[r, :] - mi[0:1, :]) * mi[1:2, :]
        slope = slope_of(n * gain[...] + bias[...])[1]
        value = d[r, :] * mask[r, :] * slope
        d[r, :] = value
        return carry[0] + fold(value), carry[1] + fold(value * n)

    both = over_rows(z.shape[0], one, (zero, zero))
    sums[0:1, :] = column_sum(both[0])
    sums[1:2, :] = column_sum(both[1])


def unmix_kernel(place, number, d2, q0, q1, q2, q3, z2, mi2, gain2, mask, z1, mi1, gain1, bias1, ka, kt, dz2, d1, sums, tot, gs):
    merged_sums((q0, q1, q2, q3), tot)
    clear_borders(gs)
    images = gs.shape[0]
    rows, width = z2.shape
    half = width // 2
    column = frame_column(128)

    def one(image, carry):
        r = pl.ds(pl.multiple_of(image * PIX, PIX), PIX)
        for j in range(width // 128):
            cols = pl.ds(j * 128, 128)
            g = gain2[:, cols] * mi2[1:2, cols]
            c1 = g * tot[0:1, cols] / number[0:1, 0:1]
            c2 = g * tot[1:2, cols] / number[0:1, 0:1]
            n = (z2[r, cols] - mi2[0:1, cols]) * mi2[1:2, cols]
            d = mask[r, :] * (g * d2[r, cols] - (c1 + n * c2))
            dz2[r, cols] = d.astype(bf16)
            for k, copy in enumerate(shifted_copies(d, column)):
                gs[image, PAD : PAD + PIX, pl.ds(k * width + j * 128, 128)] = copy.astype(bf16)
        return carry

    lax.fori_loop(0, images, one, 0)
    for d in range(3):
        for k in range(3):
            moved = gs[:, FRAME * (2 - d) : FRAME * (2 - d) + PIX, pl.ds((2 - k) * width, width)]
            moved = moved.reshape(rows, width)
            tap = pl.ds((3 * d + k) * half, half)
            for side, kernel in enumerate((ka, kt)):
                cols = pl.ds(side * half, half)
                part = lax.dot_general(moved, kernel[tap, :], last_only, preferred_element_type=f32)
                d1[:, cols] = part if d + k == 0 else d1[:, cols] + part
    narrow_back(d1, z1, mi1, gain1, bias1, mask, sums)


def narrow_finish(d1, q, z1, mi1, gain1, mask, number, dz1, tot):
    merged_sums(q, tot)
    g = gain1[...] * mi1[1:2, :]
    c1 = g * tot[0:1, :] / number[0:1, 0:1]
    c2 = g * tot[1:2, :] / number[0:1, 0:1]

    def one(r, carry):
        n = (z1[r, :] - mi1[0:1, :]) * mi1[1:2, :]
        dz1[r, :] = (mask[r, :] * (g * d1[r, :] - (c1 + n * c2))).astype(bf16)
        return carry

    over_rows(z1.shape[0], one, 0)


def widen_kernel(place, number, d1, q0, q1, q2, q3, z1, mi1, gain1, mask, ds, z3, mi3, gain3, bias3, u, w, dz1, ds0, sums, tot, du):
    narrow_finish(d1, (q0, q1, q2, q3), z1, mi1, gain1, mask, number, dz1, tot)
    for i, cols in enumerate(blocks(ds.shape[1])):
        du[...] = lax.dot_general(dz1[...], w[cols, :], last_only, preferred_element_type=f32)

        def one(r, carry, cols=cols):
            dy = (du[r, :] + ds[r, cols].astype(f32)).astype(bf16).astype(f32)
            n = (z3[r, cols].astype(f32) - mi3[0:1, cols]) * mi3[1:2, cols]
            s = n * gain3[:, cols] + bias3[:, cols] + u[r, cols].astype(f32)
            d = dy * mask[r, :] * slope_of(s)[1]
            ds0[r, cols] = d.astype(bf16)
            return carry[0] + fold(d), carry[1] + fold(d * n)

        zero = jnp.zeros((8, cols.size), f32)
        both = over_rows(ds.shape[0], one, (zero, zero))
        sums[0:1, cols] = column_sum(both[0])
        sums[1:2, cols] = column_sum(both[1])


def last_kernel(place, number, d1, q0, q1, q2, q3, z1, mi1, gain1, mask, ds, w, dz1, keep, give, tot):
    narrow_finish(d1, (q0, q1, q2, q3), z1, mi1, gain1, mask, number, dz1, tot)
    half = keep.shape[0]
    for i, cols in enumerate(blocks(ds.shape[1])):
        block = lax.dot_general(dz1[...], w[cols, :], last_only, preferred_element_type=f32)
        keep[:, cols] = block[:half] + ds[:half, cols].astype(f32)
        give[:, cols] = (block[half:] + ds[half:, cols].astype(f32)).astype(bf16)


def in_place_kernel(where, mine, other, out):
    core, y_side = where[0], where[2]
    size = mine.shape[0] // 2
    for source, side in ((mine, core), (other, 1 - core)):
        for y in range(2):
            at = pl.multiple_of((side * 2 + (y ^ y_side)) * size, 16)
            out[pl.ds(at, size), :] = source[pl.ds(y * size, size), :].astype(f32)


def first_mix_kernel(shares, where, *refs):
    give, keep = refs[-2:]
    core, x_side, y_side = where[0], where[1], where[2]
    for section in range(2):
        for half in range(2):
            kept = jnp.where(core == 0, section == x_side, half == y_side)
            at = jnp.where(core == 0, half, section)
            for out, chosen in ((keep, kept), (give, jnp.logical_not(kept))):

                @pl.when(chosen)
                def _(out=out, at=at, section=section, half=half):
                    start = 0
                    for k, share in enumerate(shares):
                        own, other = refs[4 * k + 2 * section : 4 * k + 2 * section + 2]
                        rows = pl.ds(half * share, share)
                        value = own[rows, :].astype(f32) + other[rows, :].astype(f32)
                        out[at, pl.ds(start, share), :] = value.astype(bf16)
                        start += share


def second_mix_kernel(where, keep, got, give_out, keep_out):
    for at in range(2):
        for out, chosen in ((keep_out, at == where[0]), (give_out, at != where[0])):

            @pl.when(chosen)
            def _(out=out):
                out[...] = (keep[at].astype(f32) + got[at].astype(f32)).astype(bf16)


def drop_kernel(codes, cots, head, merged):
    line = lax.broadcasted_iota(jnp.int32, cots.shape[1:], 0)
    bounds = (0, KSEG, KSEG + KDEP, KSEG + KDEP + KNOR)
    cot = cots[0].astype(f32)
    tasks = [
        jnp.where((line >= a) & (line < b), cot, 0.0).T.astype(bf16)
        for a, b in zip(bounds[:-1], bounds[1:])
    ]
    for cols in blocks(head.shape[1], 8):
        g = [jnp.dot(task, head[:, cols], preferred_element_type=f32) for task in tasks]
        total = g[0] + g[1] + g[2]
        magnitude = sum(jnp.sqrt(v * v + DROP_FLOOR * DROP_FLOOR) for v in g)
        purity = 0.5 + 0.5 * (total / magnitude)
        bar = (codes[0, :, cols] + 0.5) / CODE_SCALE
        keep = sigmoid((purity - bar) * DROP_SHARPNESS)
        lose = 1.0 - keep
        value = sum(v * jnp.where(v > 0.0, keep, lose) for v in g)
        merged[:, cols] = value.astype(bf16)


VM = pl.BlockSpec(memory_space=pltpu.VMEM)
SM = pl.BlockSpec(memory_space=pltpu.SMEM)
ANY = pl.BlockSpec(memory_space=pltpu.HBM)


def run(kernel, operands, specs, outs, scratch, flops):
    return pl.pallas_call(
        kernel,
        out_shape=[jax.ShapeDtypeStruct(shape, kind) for shape, kind in outs],
        in_specs=specs,
        out_specs=[VM] * len(outs),
        scratch_shapes=scratch,
        compiler_params=pltpu.CompilerParams(vmem_limit_bytes=LIMIT),
        cost_estimate=pl.CostEstimate(
            flops=SCALE * flops,
            bytes_accessed=SCALE * sum(o.size * o.dtype.itemsize for o in operands[:16]),
            transcendentals=0,
        ),
    )(*operands)


def flip(value, bits):
    count = lax.axis_size("dp")
    return lax.ppermute(value, "dp", [(i, i ^ bits) for i in range(count)])


def cross(value, bits):
    count = lax.axis_size("segment")
    return lax.ppermute(value, "segment", [(i, i ^ bits) for i in range(count)])


def turned(value, even, odd):
    size, count = lax.axis_size("segment"), lax.axis_size("dp")
    pairs = [
        (i * count + j, (i ^ (odd if j % 2 else even)) * count + j) for i in range(size) for j in range(count)
    ]
    return lax.ppermute(value, ("segment", "dp"), pairs)


def after(value, *others):
    return lax.optimization_barrier((value,) + others)[0]


def dp_bits():
    count = lax.axis_size("dp")
    return [1 << k for k in range(count.bit_length() - 1)]


def group_bits():
    bits = [b for b in dp_bits() if b != SWAP]
    return bits[:2], bits[2:]


def four_parts(value):
    first, _ = group_bits()
    near = jnp.stack([value, flip(value, first[0])])
    far = flip(near, first[1])
    return [near[0], near[1], far[0], far[1]]


def pair_up(stats, count):
    for b in group_bits()[1]:
        other, other_count = flip(stats, b), flip(count, b)
        whole = count + other_count
        here, there = count[0, 0], other_count[0, 0]
        away = stats[0] / here - other[0] / there
        square = stats[1] + other[1] + away * away * (here * there / (here + there))
        merged = jnp.stack([stats[0] + other[0], square])
        if stats.shape[0] > 2:
            merged = jnp.concatenate([merged, stats[2:] + other[2:]], axis=0)
        stats, count = merged, whole
    return stats


def pair_sum(value):
    for b in group_bits()[1]:
        value = value + flip(value, b)
    return value


def split_rows(value, index, parts=2):
    size = value.shape[0] // parts
    return lax.dynamic_slice_in_dim(value, index * size, size, 0)


def on_device(
    inputs,
    extents,
    wide_weight,
    mid_weight,
    narrow_gain,
    narrow_bias,
    expand_gain,
    expand_bias,
    head_weight,
    head_cotangent,
    drop_codes,
):
    seg = lax.axis_index("segment")
    dp = lax.axis_index("dp")
    sections = lax.axis_size("segment")
    x_side, y_side, core = seg % 2, seg // 2, dp % 2
    swapped = (dp // SWAP) % 2
    channels = inputs.shape[-1]
    narrow = wide_weight.shape[-1]
    half_width = narrow // 2
    classes = head_weight.shape[-1]
    place = jnp.stack([seg, core]).astype(jnp.int32)

    own_small = jnp.concatenate(
        [head_weight.T, jnp.zeros((HEADS - classes, head_weight.shape[0]), bf16), expand_gain.T, expand_bias.T]
        + [narrow_gain, narrow_bias, jnp.zeros((10, narrow), bf16)],
        axis=0,
    )
    small_x = cross(own_small, 1)
    small_y = cross(jnp.stack([own_small, small_x]), 2)
    small = jnp.stack([own_small, small_x, small_y[0], small_y[1]])
    small = jnp.stack([lax.dynamic_index_in_dim(small, k ^ seg, 0, keepdims=False) for k in range(4)])
    lanes = jnp.moveaxis(small[:, : HEADS + 4], 0, 1).reshape(HEADS + 4, channels)
    head_rows = lanes[:HEADS]
    gain_wide = lanes[HEADS : HEADS + 2].astype(f32)
    bias_wide = lanes[HEADS + 2 : HEADS + 4].astype(f32)
    gain_narrow = small[:, HEADS + 4].astype(f32)
    bias_narrow = small[:, HEADS + 5].astype(f32)

    own_count = inputs.shape[0]
    start = seg * own_count

    def own_part(value):
        return lax.dynamic_slice_in_dim(value, start, own_count, 0).astype(f32).reshape(own_count, -1, PIX)

    boxes = jnp.pad(extents, ((0, 0), (0, 0), (0, PIX - 2)))
    facts = jnp.concatenate([own_part(v) for v in (head_cotangent, drop_codes, boxes)], axis=1)
    facts = jnp.pad(facts, ((0, 0), (0, -facts.shape[1] % 8), (0, 0)))
    keep_facts = lax.dynamic_index_in_dim(facts, swapped, 0, keepdims=False)
    got_facts = flip(lax.dynamic_index_in_dim(facts, 1 - swapped, 0, keepdims=False), SWAP)
    facts = jnp.stack([keep_facts, got_facts])
    code_rows = channels // PIX
    cotangent = facts[:, :classes].astype(bf16)
    codes = facts[:, classes : classes + code_rows].reshape(2, 1, channels)
    box = facts[:, classes + code_rows, :2].astype(jnp.int32)
    keep_in = lax.dynamic_index_in_dim(inputs, swapped, 0, keepdims=False)
    give_in = lax.dynamic_index_in_dim(inputs, 1 - swapped, 0, keepdims=False)
    half_pix = PIX // 2
    got_in = [flip(give_in[:, :half_pix], SWAP)]
    images = 2 * inputs.shape[1]
    rows = images * PIX

    wide_own = wide_weight[0]
    mid_own = mid_weight[0].reshape(-1, narrow)

    def exchange(own, *gate):
        mine = split_rows(own, core)
        mine = after(mine, *gate) if gate else mine
        return turned(mine, 1, 2), turned(mine, 2, 1)

    def pass_on(own, first, second, gate, flip_gate=()):
        pieces = [first, second, turned(after(first, second, *gate), 2, 1)]
        return [own] + pieces + [flip(after(p, *flip_gate), 1) for p in pieces]

    wide = pass_on(wide_own, *exchange(wide_own), (got_in[0], small_x, got_facts))
    got_in.append(flip(after(give_in[:, half_pix:], got_in[0], wide[4], wide[5]), SWAP))
    mid_two = exchange(mid_own, wide[1], wide[2])

    local_count = jnp.full((8, 128), jnp.sum(box[:, 0] * box[:, 1]).astype(f32))
    position = jnp.arange(PIX, dtype=jnp.int32)
    inside = (position // FRAME < box[:, 0:1]) & (position % FRAME < box[:, 1:2])
    mask = inside.astype(f32).reshape(rows, 1)

    cot_columns = jnp.pad(cotangent, ((0, 0), (0, HEADS - classes), (0, 0)))
    (merged,) = pl.pallas_call(
        drop_kernel,
        grid=(images,),
        in_specs=[
            pl.BlockSpec((1, 1, channels), lambda i: (i, 0, 0)),
            pl.BlockSpec((1, HEADS, PIX), lambda i: (i, 0, 0)),
            pl.BlockSpec((HEADS, channels), lambda i: (0, 0)),
        ],
        out_specs=[pl.BlockSpec((PIX, channels), lambda i: (i, 0))],
        out_shape=[jax.ShapeDtypeStruct((rows, channels), bf16)],
        compiler_params=pltpu.CompilerParams(vmem_limit_bytes=LIMIT),
    )(codes, cot_columns, head_rows)

    got_in = jnp.concatenate([got_in[0], after(got_in[1], merged)], axis=1)
    entry = jnp.concatenate([keep_in, got_in], axis=0).reshape(rows, channels)

    narrow_f = ((rows, narrow), f32)
    narrow_b = ((rows, narrow), bf16)
    wide_f = ((rows, channels), f32)
    wide_b = ((rows, channels), bf16)
    pair_n = ((2, narrow), f32)
    pair_w = ((2, channels), f32)
    copies_b = ((images, PIX + 2 * PAD, 3 * narrow), bf16)
    w_out = ((channels, narrow), bf16)
    m_out = ((9 * half_width, narrow), bf16)
    w_scratch = [None, pltpu.SemaphoreType.DMA((4,))]
    m_scratch = [pltpu.SemaphoreType.DMA((4,)), pltpu.SemaphoreType.DMA((4,))]
    w_specs = [ANY] * 7
    product = 2 * rows * channels * narrow
    conv = 2 * rows * 9 * narrow * narrow

    def row(values, k):
        return values[k : k + 1]

    met = {}

    def moments(stats):
        if id(stats) not in met:
            met[id(stats)] = (four_parts(pair_up(stats, local_count)), stats)
        return met[id(stats)][0]

    kept = {}
    z1, st, w_head = run(
        functools.partial(first_kernel, 0),
        [place, local_count, entry, mask] + wide,
        [SM, VM, VM, VM] + w_specs,
        [narrow_f, ((8, narrow), f32), w_out],
        w_scratch[1:],
        product,
    )
    group_counts = moments(st)
    mid = pass_on(mid_own, *mid_two, (merged, z1), group_counts)
    number = sum(g[2:3, :128] for g in group_counts)
    group_counts = [g[2:3, :128] for g in group_counts]
    u = entry
    for k in range(2):
        head, tail = 2 * k, 2 * k + 1
        hs, z2, st2, mi1, ka, kt = run(
            functools.partial(middle_kernel, head),
            [place] + group_counts + [z1] + moments(st) + [row(gain_narrow, head), row(bias_narrow, head), mask] + mid,
            [SM] + [VM] * 12 + w_specs,
            [copies_b, narrow_f, pair_n, pair_n, m_out, m_out],
            m_scratch,
            conv,
        )
        h2, z3, st3, mi2, w_tail = run(
            functools.partial(expand_kernel, tail),
            [place] + group_counts + [z2] + moments(st2) + [row(gain_narrow, tail), row(bias_narrow, tail), mask] + wide,
            [SM] + [VM] * 12 + w_specs,
            [narrow_b, wide_b, pair_w, pair_n, w_out],
            [pltpu.VMEM((rows, channels // 4), f32), w_scratch[1]],
            product,
        )
        kept[k] = dict(z1=z1, mi1=mi1, hs=hs, z2=z2, mi2=mi2, h2=h2, z3=z3, u=u, ka=ka, kt=kt, w_head=w_head, w_tail=w_tail)
        last = [row(gain_wide, k), row(bias_wide, k), u, mask]
        if k == 0:
            u, z1, st, kept[0]["mi3"], w_head = run(
                functools.partial(join_kernel, 2),
                [place] + group_counts + [z3] + moments(st3) + last + wide,
                [SM] + [VM] * 13 + w_specs,
                [wide_b, narrow_f, pair_n, pair_w, w_out],
                w_scratch[1:],
                product,
            )
        else:
            ds, sums3, logits, head_grad, mi3 = run(
                turn_kernel,
                group_counts + [z3] + moments(st3) + last + [merged, head_rows, cot_columns],
                [VM] * 16,
                [wide_b, pair_w, ((HEADS, rows), f32), ((2, 4, HEADS // 2, channels // 4), bf16), pair_w],
                [pltpu.VMEM((rows, channels // 4), bf16)],
                product // 4,
            )
            kept[1]["mi3"] = mi3

    grads, totals = {}, {}

    def plus(a, b):
        return (a.astype(f32) + b.astype(f32)).astype(bf16)

    def joined(side, mine, other):
        return jnp.where(
            side == 1, jnp.concatenate([other, mine], axis=0), jnp.concatenate([mine, other], axis=0)
        )

    second_side = jnp.where(core == 0, y_side, x_side).astype(jnp.int32)
    sides = jnp.stack([core, x_side, y_side]).astype(jnp.int32)

    class Chain:
        def __init__(self, kinds):
            shares = tuple(kind[0].shape[0] // 2 for kind in kinds)
            shape = jax.ShapeDtypeStruct((2, sum(shares), narrow), bf16)
            operands = [value for kind in kinds for value in kind]
            self.give, self.keep = pl.pallas_call(
                functools.partial(first_mix_kernel, shares),
                in_specs=[SM] + [VM] * len(operands),
                out_specs=[VM, VM],
                out_shape=[shape, shape],
                compiler_params=pltpu.CompilerParams(vmem_limit_bytes=LIMIT),
            )(sides, *operands)
            self.todo = ["first", "second"]
            self.todo += ["in", "mid", "out"] if z_chips == 4 else [("meet", b) for b in dp_bits()[1:]]

        def send(self):
            step = self.todo.pop(0)
            if step == "first":
                self.got = turned(self.give, 1, 2)
            elif step == "second":
                self.got = turned(self.give, 2, 1)
            elif isinstance(step, tuple):
                self.got = flip(self.part, step[1])
            else:
                ways = {"in": [(0, 1), (3, 2)], "mid": [(1, 2), (2, 1)], "out": [(1, 0), (2, 3)]}[step]
                self.got = line_send(self.part, ways)
            self.step = step
            return self.got

        def take(self, *holds):
            got = after(self.got, *holds)
            if self.todo[:1] == ["second"]:
                shape = jax.ShapeDtypeStruct(got.shape[1:], bf16)
                self.give, self.keep = pl.pallas_call(
                    second_mix_kernel,
                    in_specs=[SM, VM, VM],
                    out_specs=[VM, VM],
                    out_shape=[shape, shape],
                    compiler_params=pltpu.CompilerParams(vmem_limit_bytes=LIMIT),
                )(second_side.reshape(1), self.keep, got)
                return self.give
            if self.step == "second":
                self.part = plus(self.keep, got)
            elif self.step == "out":
                self.part = jnp.where((z_place == 1) | (z_place == 2), self.part, got)
            else:
                self.part = plus(self.part, got)
            return self.part

    z_chips = lax.axis_size("dp") // 2
    z_place = dp // 2

    def line_send(value, ways):
        return lax.ppermute(value, "dp", [(2 * a + c, 2 * b + c) for a, b in ways for c in range(2)])

    def to_owner(part, part1):
        keep = jnp.where(y_side == 0, part, part1)
        return jnp.concatenate([keep, cross(jnp.where(y_side == 0, part1, part), 2)])

    def in_place(half):
        (out,) = pl.pallas_call(
            in_place_kernel,
            in_specs=[SM, VM, VM],
            out_specs=[VM],
            out_shape=[jax.ShapeDtypeStruct((2 * half.shape[0], narrow), f32)],
            compiler_params=pltpu.CompilerParams(vmem_limit_bytes=LIMIT),
        )(sides, half, flip(half, 1))
        return out

    def tile_grad(left, right, dims=rows_only):
        return lax.dot_general(left, right, dims, preferred_element_type=f32).astype(bf16)

    def conv_grad(hs, dz2, side):
        right = dz2.reshape(images, PIX, narrow)
        both = (((0, 1), (0, 1)), ((), ()))
        width = 3 * half_width
        parts = [
            tile_grad(hs[:, FRAME * d : FRAME * d + PIX, side * width : (side + 1) * width], right, both)
            for d in range(3)
        ]
        whole = jnp.concatenate(parts, axis=0)
        return split_rows(whole, core), flip(split_rows(whole, 1 - core), 1)

    def sections_of(kind, k):
        return [v for i in range(2) for v in grads[kind, 2 * k + i]]

    def split_grad(left, right):
        size = left.shape[1] // 2
        mine, other = [tile_grad(lax.dynamic_slice_in_dim(left, c * size, size, 1), right) for c in (core, 1 - core)]
        return mine, flip(other, 1)

    for k in (1, 0):
        head, tail = 2 * k, 2 * k + 1
        it = kept[k]
        narrow2 = [it["z2"], it["mi2"], row(gain_narrow, tail)]
        narrow1 = [it["z1"], it["mi1"], row(gain_narrow, head)]
        dz3, d2, sums2, totals["wide", k] = run(
            shrink_kernel,
            [place if k else first_hold, number, ds, it["z3"]] + four_parts(pair_sum(sums3)) + [it["mi3"], row(gain_wide, k), mask]
            + narrow2 + [row(bias_narrow, tail), it["w_tail"]],
            [SM] + [VM] * 15,
            [wide_b, narrow_f, pair_n, pair_w],
            [],
            product,
        )
        grads["w", tail] = split_grad(dz3, it["h2"])
        parts2 = four_parts(pair_sum(sums2))
        hold = place
        if k == 0:
            hold = after(place, m1.take(), w1.take(m1.part))
            w1.send()
        dz2, d1, sums1, totals["narrow", tail] = run(
            unmix_kernel,
            [hold, number, d2] + parts2 + narrow2 + [mask] + narrow1
            + [row(bias_narrow, head), it["ka"], it["kt"]],
            [SM] + [VM] * 16,
            [narrow_b, narrow_f, pair_n, pair_n],
            [pltpu.VMEM(*copies_b)],
            conv,
        )
        parts1 = four_parts(pair_sum(sums1))
        grads["m", head] = conv_grad(it["hs"], dz2, 0)
        grads["m", tail] = conv_grad(it["hs"], dz2, 1)
        hold = place
        if k == 1:
            m1 = Chain([sections_of("m", 1)])
            m1.send()
            hold = after(place, m1.give)
        else:
            m0 = Chain([sections_of("m", 0)])
            hold = after(place, w1.take(), m0.give)
            m1.part = after(m1.part, *parts1)
            m1.send()
            m0.send()
        base = [hold, number, d1] + parts1 + narrow1 + [mask, ds]
        if k == 1:
            low = kept[0]
            dz1, ds, sums3, totals["narrow", head] = run(
                widen_kernel,
                base + [low["z3"], low["mi3"], row(gain_wide, 0), row(bias_wide, 0), low["u"], it["w_head"]],
                [SM] + [VM] * 17,
                [narrow_b, wide_b, pair_w, pair_n],
                [pltpu.VMEM((rows, channels // 4), f32)],
                product,
            )
            grads["w", head] = split_grad(it["u"], dz1)
        else:
            dz1, grad_keep, grad_give, totals["narrow", head] = run(
                last_kernel,
                base + [it["w_head"]],
                [SM] + [VM] * 12,
                [narrow_b, ((rows // 2, channels), f32), ((rows // 2, channels), bf16), pair_n],
                [],
                product,
            )
            grads["w", head] = split_grad(it["u"], dz1)
        if k == 1:
            own = lax.dynamic_index_in_dim(head_grad, core, 0, keepdims=False)
            other = flip(lax.dynamic_index_in_dim(head_grad, 1 - core, 0, keepdims=False), 1)
            extra = [v[2 * i : 2 * i + 2].reshape(-1, narrow) for i in range(2) for v in (own, other)]
            w1 = Chain([sections_of("w", 1), extra])
            w1.send()
            first_hold = after(place, m1.take(), w1.give)
            m1.send()
    flat = jnp.concatenate(
        [totals["wide", k].reshape(-1, narrow) for k in range(2)]
        + [totals["narrow", i] for i in range(sections)],
        axis=0,
    )
    def returned(keep, got):
        got = got.astype(f32)
        return jnp.stack([jnp.where(swapped == 0, keep, got), jnp.where(swapped == 0, got, keep)])

    by_pair = z_chips == 4 and SWAP == 2
    home = line_send(grad_give, [(1, 0), (2, 3)]) if by_pair else flip(grad_give, SWAP)
    w0 = Chain([sections_of("w", 0)])
    w0.send()
    tick = m0.take(w0.give)
    m0.send()
    w1.part = after(w1.part, tick)
    w1.send()
    tick = m1.take(w1.part)
    m1.send()
    tick = m0.take(tick)
    m0.send()
    tick = w0.take(tick)
    w0.send()
    tick = m1.take(tick, home)
    m1.send()
    tick = w1.take(tick)
    w1.send()
    tick = w0.take(tick)
    w0.send()
    tick = m0.take(tick)
    m0.send()
    if by_pair:
        back = line_send(after(grad_give, tick), [(0, 1), (3, 2)])
        home = jnp.where((z_place == 0) | (z_place == 3), home, back)
    flat = after(flat, tick)
    flat = flat + cross(flat, 1)
    tick = m1.take(tick)
    tick = w1.take(tick)
    w1.send()
    tick = w0.take(tick, flat)
    w0.send()
    flat = flat + cross(flat, 2)
    tick = m0.take(tick)
    m0.send()
    tick = w1.take(tick)
    edge = wide_own.shape[0] // 4
    heads = joined(core, w1.part[edge:], flip(w1.part[edge:], 1))
    tick = w0.take(tick, flat)
    w0.send()
    by_image = after(logits, tick)[:classes].reshape(classes, images, PIX).transpose(1, 0, 2)
    logits_out = returned(by_image[: images // 2], flip(by_image[images // 2 :].astype(bf16), SWAP))
    flat = flat + flip(after(flat, tick), SWAP)
    tick = m0.take(tick, heads)
    mid_half = to_owner(m0.part, m1.part)
    shape = (images // 2, PIX, channels)
    input_grad = returned(grad_keep.reshape(shape), after(home, tick).reshape(shape))
    wide_half = to_owner(w0.take(tick), w1.part[:edge])
    mid_grad = in_place(mid_half)
    wide_grad = in_place(wide_half)

    wide_count = 4 * channels // narrow
    wide_all = flat[:wide_count].reshape(2, 2, channels)
    narrow_all = lax.dynamic_index_in_dim(
        flat[wide_count:].reshape(sections, 2, narrow), seg, 0, keepdims=False
    )
    share = channels // sections
    wide_mine = lax.dynamic_slice_in_dim(wide_all, seg * share, share, 2)

    head_out = heads[:classes].astype(f32).T

    return (
        logits_out,
        input_grad,
        wide_grad[None],
        mid_grad.reshape(1, 9, half_width, narrow),
        narrow_all[1:2],
        narrow_all[0:1],
        wide_mine[:, 1].T,
        wide_mine[:, 0].T,
        head_out,
    )


def solution(mesh):
    return jax.shard_map(
        on_device,
        mesh=mesh,
        in_specs=(
            P("segment", "dp", None, None),
            P(None, "dp", None),
            P("segment", None, None),
            P("segment", None, None, None),
            P("segment", None),
            P("segment", None),
            P("segment", None),
            P("segment", None),
            P("segment", None),
            P(None, "dp", None, None),
            P(None, "dp", None),
        ),
        out_specs=(
            P("segment", "dp", None, None),
            P("segment", "dp", None, None),
            P("segment", None, None),
            P("segment", None, None, None),
            P("segment", None),
            P("segment", None),
            P("segment", None),
            P("segment", None),
            P("segment", None),
        ),
        check_vma=False,
    )
```
